256 devices in a mesh: dp: 64 (over z, y, x_hi), seq: 4 (over x_lo, core).
Axes of the slice: x: 4 (x_hi: 2, x_lo: 2; x = x_hi * 2 + x_lo), y: 4, z: 8, core: 2. Of those that a mesh axis runs over, the one named last changes fastest.
Arguments:
- queries: bfloat16 [64, 1024, 1024], P('dp', 'seq'), may hold values from -5 to 5
- keys: bfloat16 [64, 1024, 1024], P('dp', 'seq'), may hold values from -5 to 5
- values: bfloat16 [64, 1024, 1024], P('dp', 'seq'), may hold values from -16 to 16
- segment_ids: int32 [64, 1024], P('dp', 'seq'), may hold values from 0 to 7, never falling along the last dimension, each value on 1 to 512 neighbouring positions
- out_weight: bfloat16 [1024, 2048], replicated, may hold values from -0.1875 to 0.1875
- out_grad: bfloat16 [64, 1024, 2048], P('dp', 'seq'), may hold values from -6 to 6
Outputs:
- projected: bfloat16 [64, 1024, 2048], P('dp', 'seq')
- query_grad: bfloat16 [64, 1024, 1024], P('dp', 'seq')
- key_grad: bfloat16 [64, 1024, 1024], P('dp', 'seq')
- value_grad: bfloat16 [64, 1024, 1024], P('dp', 'seq')
- weight_grad: bfloat16 [1024, 2048], P('dp')
The draws below stay inside these ranges and needn't reach their ends.
Inputs may be any that keep to these rules, and one draw needn't show every extreme that they name: `segment_ids`: each row holds 8 documents in order, the longest exactly 512 positions.
All inputs are finite; a program needn't handle non-finite values.
Results may differ from the reference program's by a relative error of at most 0.029.
Values may be sent and summed in bfloat16 or wider, within the bound.
A program may use at most 128 MiB of HBM per device.

```python
import math
import jax
import jax.numpy as jnp
import numpy as np
from jax import lax

D = 2048
HEADS = 8
HEAD = 128
HD = 1024
SEQ_LEN = 1024
ROWS = 64
DOCS = 8
DOC_MOST = 512


def draw_queries(key, part):
    key = jax.random.fold_in(key, 1)
    base = jnp.clip(jax.random.normal(key, (ROWS, SEQ_LEN, HD), jnp.float32), -4.0, 4.0)
    return base.astype(jnp.bfloat16)


def draw_keys(key, part):
    key = jax.random.fold_in(key, 2)
    base = jnp.clip(jax.random.normal(key, (ROWS, SEQ_LEN, HD), jnp.float32), -4.0, 4.0)
    return base.astype(jnp.bfloat16)


def strengthened(drawn, stream_key, source, target, shards_of, factor):
    owner, partner = [(jnp.arange(drawn.shape[dim]) // (drawn.shape[dim] // shards_of)).reshape([-1 if axis == dim else 1 for axis in range(drawn.ndim)]) for dim in (source, target)]
    chosen = jax.random.permutation(stream_key, shards_of)[partner]
    strong = (owner == chosen) | (owner == (partner + shards_of // 2) % shards_of)
    return jnp.where(strong, factor * drawn, drawn)


def block_scale(key, dims, cuts, least, top_value):
    loudness, own = 1.0, jax.random.fold_in(key, 6)
    for position, shards_of in cuts:
        draws = jnp.exp(jax.random.uniform(jax.random.fold_in(own, position), (shards_of,), jnp.float32, least / len(cuts), top_value / len(cuts)))
        loudness = loudness * jnp.repeat(draws, dims[position] // shards_of).reshape([-1 if axis == position else 1 for axis in range(len(dims))])
    return loudness


def length_profile(amount, total, most, lean):
    loads = [(1 << 20) // math.isqrt(rank ** lean) + 1 for rank in range(2, amount + 1)]
    surplus, given = total - most - (amount - 1), [1] * (amount - 1)
    while surplus > 0:
        movable = [i for i in range(amount - 1) if given[i] < most]
        whole, left = sum([loads[i] for i in movable]), surplus
        for i in movable:
            addition = min(most - given[i], max(1, left * loads[i] // whole), surplus)
            given[i] = given[i] + addition
            surplus = surplus - addition
    return np.array([most] + given)


def uneven(own_key, number_of, total, limit, slope):
    if number_of == 2:
        one = jax.random.randint(own_key, (), max(1, total - limit), min(limit, total - 1) + 1)
        return jnp.stack([one, total - one])
    sizes = jnp.asarray(length_profile(number_of, total, limit, slope), jnp.int32)
    twos = (number_of - 1) // 2
    giver, receiver = sizes[1:1 + 2 * twos:2], sizes[2:2 + 2 * twos:2]
    margin = jnp.minimum(giver - 1, limit - receiver)
    shifted = jax.random.randint(jax.random.fold_in(own_key, 1), (twos,), 0, 1 << 20) % (margin + 1)
    sizes = sizes.at[1:1 + 2 * twos:2].set(giver - shifted).at[2:2 + 2 * twos:2].set(receiver + shifted)
    return sizes[jax.random.permutation(jax.random.fold_in(own_key, 2), number_of)]


def normal_values(own_key, shape, spread, most, pieces=(), kind=jnp.bfloat16):
    level = block_scale(own_key, shape, pieces, -0.22, 0.18) if pieces else 1.0
    result = jax.random.normal(own_key, shape, jnp.float32) * spread * level
    return jnp.minimum(jnp.maximum(result, -most), most).astype(kind)


def heavy_noise(key, shape, scale, most, cuts, heavy, kind=jnp.bfloat16):
    values = scale * jax.random.normal(key, shape, jnp.float32)
    if cuts:
        values = values * block_scale(key, shape, cuts, -0.22, 0.18)
    return jnp.clip(strengthened(values, jax.random.fold_in(key, 3), *heavy), -most, most).astype(kind)


def setup_inputs(seed: int = 0) -> dict:
    key_list = jax.random.split(jax.random.key(seed), 7)
    return {
        "queries": draw_queries(jax.random.fold_in(key_list[6], 71), 0),
        "keys": draw_keys(jax.random.fold_in(key_list[6], 71), 0),
        "values": heavy_noise(key_list[2], (ROWS, SEQ_LEN, HD), 1.0, 16.0, ((0, 64), (1, 4)), (0, 2, 64, 4.0)),
        "segment_ids": jax.vmap(lambda own: jnp.searchsorted(jnp.cumsum(uneven(own, DOCS, SEQ_LEN, DOC_MOST, 2)), jnp.arange(SEQ_LEN), side="right"))(jax.random.split(key_list[3], ROWS)).reshape((ROWS, SEQ_LEN)).astype(jnp.int32),
        "out_weight": normal_values(key_list[4], (HD, D), HD ** -0.5, 0.1875),
        "out_grad": normal_values(key_list[5], (ROWS, SEQ_LEN, D), 1.0, 6.0, ((0, 64), (1, 4))),
    }


def attention_weights(query_heads, key_heads, query_places, key_places, query_docs, key_docs):
    scores = jnp.einsum('qhe,khe->hqk', query_heads.astype(jnp.float32), key_heads.astype(jnp.float32)) * (HEAD ** -0.5)
    visible = (key_places[None, :] <= query_places[:, None]) & (query_docs[:, None] == key_docs[None, :])
    scores = jnp.where(visible[None], scores, -1e30)
    row_top = jnp.max(scores, axis=2, keepdims=True)
    raised = jnp.exp(scores - row_top)
    return raised / jnp.sum(raised, axis=2, keepdims=True)


def reference(queries, keys, values, segment_ids, out_weight, out_grad):
    places = jnp.arange(SEQ_LEN, dtype=jnp.int32)
    factor = HEAD ** -0.5

    def one_row(weight_total, row_data):
        query_row, key_row, value_row, doc_row, grad_row = row_data
        query_heads = query_row.reshape(SEQ_LEN, HEADS, HEAD).astype(jnp.float32)
        key_heads = key_row.reshape(SEQ_LEN, HEADS, HEAD).astype(jnp.float32)
        value_heads = value_row.reshape(SEQ_LEN, HEADS, HEAD).astype(jnp.float32)
        weights_full = attention_weights(query_heads, key_heads, places, places, doc_row, doc_row)
        weights_low = weights_full.astype(jnp.bfloat16).astype(jnp.float32)
        attended = jnp.einsum('hqk,khe->qhe', weights_low, value_heads).astype(jnp.bfloat16)
        attended_flat = attended.reshape(SEQ_LEN, HD)
        projected = jnp.dot(attended_flat, out_weight, preferred_element_type=jnp.float32).astype(jnp.bfloat16)
        attended_grad = jnp.dot(grad_row, out_weight.T, preferred_element_type=jnp.float32).astype(jnp.bfloat16)
        grad_heads = attended_grad.reshape(SEQ_LEN, HEADS, HEAD).astype(jnp.float32)
        delta_rows = jnp.sum(grad_heads * attended.astype(jnp.float32), axis=2).T
        prob_grad = jnp.einsum('qhe,khe->hqk', grad_heads, value_heads)
        score_grad = (weights_full * (prob_grad - delta_rows[:, :, None])).astype(jnp.bfloat16).astype(jnp.float32)
        query_grad = (jnp.einsum('hqk,khe->qhe', score_grad, key_heads) * factor).astype(jnp.bfloat16)
        key_grad = (jnp.einsum('hqk,qhe->khe', score_grad, query_heads) * factor).astype(jnp.bfloat16)
        value_grad = jnp.einsum('hqk,qhe->khe', weights_low, grad_heads).astype(jnp.bfloat16)
        weight_total = weight_total + jnp.dot(attended_flat.T, grad_row, preferred_element_type=jnp.float32)
        return weight_total, (projected, query_grad.reshape(SEQ_LEN, HD), key_grad.reshape(SEQ_LEN, HD), value_grad.reshape(SEQ_LEN, HD))

    weight_total, outputs = lax.scan(one_row, jnp.zeros((HD, D), jnp.float32), (queries, keys, values, segment_ids, out_grad))
    projected, query_grad, key_grad, value_grad = outputs
    return projected, query_grad, key_grad, value_grad, weight_total.astype(jnp.bfloat16)
```

```python
import jax
import jax.numpy as jnp
from jax import lax
from jax.experimental import pallas as pl
from jax.experimental.pallas import tpu as pltpu
from jax.sharding import PartitionSpec as P

HEAD = 128
PLANES, RING, SIDES = 8, 4, 2
MESH = pl.DeviceIdType.MESH
F32, BF16 = jnp.float32, jnp.bfloat16
LOG2E = 1.4426950408889634


def dot(a, b, ca, cb):
    return lax.dot_general(a, b, (((ca,), (cb,)), ((), ())), preferred_element_type=F32)


def kernel(
    q_hbm, k_hbm, v_hbm, seg_ref, w_hbm, og_hbm,
    proj_out, dq_out, dk_out, dv_out, wg_out,
    q_s, kv, og, w, og2, dgrad, att, seg_own, seg_all, bias,
    dkv_own, dkv_out, dkv_in, part, y1_in, y1_sum, y2_in, z_out, z_in, x_out, x_in, fin, fin_in,
    q_sem, kv_sem, og_sem, w_sem, og2_sem, seg_send, seg_recv, ogs_send, ogs_recv,
    kv1_send, kv1_recv, kv2_send, kv2_recv, dk1_send, dk1_recv, dk2_send, dk2_recv,
    att_send, att_recv, y1_send, y1_recv, y2_send, y2_recv, z_send, z_recv,
    x_send, x_recv, f_send, f_recv,
):
    heads, toks = q_s.shape[0], q_s.shape[1]
    cols = og2.shape[1]
    rows = HEAD // RING
    share = rows // SIDES
    s = lax.axis_index("seq")
    d = lax.axis_index("dp")
    core = s % 2
    lo = s // 2
    z = d // (RING * SIDES)
    y = (d // SIDES) % RING
    hi = d % SIDES
    sib = s + 1 - 2 * core
    flip = y + 1 - 2 * (y % 2)
    mirror = RING - 1 - y
    ya = core * mirror + (1 - core) * flip
    yb = core * flip + (1 - core) * mirror
    yc = (y + 2) % RING

    def place(zz, yy, xx):
        return zz * (RING * SIDES) + yy * SIDES + xx

    def remote(src, dst, send, recv, dp, seq):
        return pltpu.make_async_remote_copy(
            src_ref=src, dst_ref=dst, send_sem=send, recv_sem=recv,
            device_id=(dp, seq), device_id_type=MESH,
        )

    def lanes(h):
        return pl.ds(pl.multiple_of(h * HEAD, HEAD), HEAD)

    def load_head(i, c):
        h = (z + 1 + i) % heads
        pltpu.make_async_copy(k_hbm.at[:, lanes(h)], kv.at[h, 2, 0], kv_sem.at[h]).start()
        pltpu.make_async_copy(v_hbm.at[:, lanes(h)], kv.at[h, 2, 1], kv_sem.at[h]).start()
        return c

    lax.fori_loop(0, heads, load_head, 0)
    og_copy = pltpu.make_async_copy(og_hbm, og, og_sem)
    w_copy = pltpu.make_async_copy(w_hbm, w, w_sem)
    og_copy.start()
    w_copy.start()

    def load_query(i, c):
        pltpu.make_async_copy(q_hbm.at[:, lanes(i)], q_s.at[i], q_sem).start()
        return c

    lax.fori_loop(0, heads, load_query, 0)
    mine = pl.ds(pl.multiple_of(core * cols, cols), cols)
    other = pl.ds(pl.multiple_of((1 - core) * cols, cols), cols)
    og2_copy = pltpu.make_async_copy(og_hbm.at[:, mine], og2.at[pl.ds(0, toks)], og2_sem)
    og2_copy.start()

    barrier = pltpu.get_barrier_semaphore()
    peers = [(d, (s + 1) % 4), (d, (s + 2) % 4), (d, (s + 3) % 4)]
    peers += [(place(z, flip, hi), s), (place(z, mirror, hi), s)]
    peers += [(place((z + i) % PLANES, y, hi), s) for i in range(1, PLANES)]
    if SIDES == 2:
        peers += [(place(z, y, 1 - hi), core), (place(z, y, 1 - hi), 2 + core)]
    for peer in peers:
        pl.semaphore_signal(barrier, inc=1, device_id=peer, device_id_type=MESH)

    seg_own[...] = jnp.broadcast_to(seg_ref[0:1, :].astype(F32), seg_own.shape)
    seg_all[2] = seg_own[...]

    @pl.when(s < 2)
    def _():
        seg_all[0] = jnp.full(seg_own.shape, -1.0, F32)

        def clear(h, c):
            kv[h, 0] = jnp.zeros((2, toks, HEAD), BF16)
            return c

        lax.fori_loop(0, heads, clear, 0)

    @pl.when(s < 1)
    def _():
        seg_all[1] = jnp.full(seg_own.shape, -1.0, F32)

        def clear(h, c):
            kv[h, 1] = jnp.zeros((2, toks, HEAD), BF16)
            return c

        lax.fori_loop(0, heads, clear, 0)

    def wait_head(h, c):
        pltpu.make_async_copy(kv.at[h, 2], kv.at[h, 2], kv_sem.at[h]).wait()
        return c

    lax.fori_loop(0, heads, wait_head, 0)
    pl.semaphore_wait(barrier, len(peers))

    def kv1(h):
        return remote(kv.at[h, 2], kv.at[h, 1], kv1_send.at[h], kv1_recv.at[h], d, (s + 1) % 4)

    def kv2(h):
        return remote(kv.at[h, 2], kv.at[h, 0], kv2_send.at[h], kv2_recv.at[h], d, (s + 2) % 4)

    def kv2_relay(h):
        return remote(kv.at[h, 1], kv.at[h, 0], kv2_send.at[h], kv2_recv.at[h], d, (s + 1) % 4)

    def send_kv(t):
        h = (z + 1 + t) % heads

        @pl.when(s < 3)
        def _():
            kv1(h).start()

        @pl.when(s == 0)
        def _():
            kv2(h).start()

    seg1 = remote(seg_own, seg_all.at[1], seg_send.at[0], seg_recv.at[0], d, (s + 1) % 4)
    seg2 = remote(seg_own, seg_all.at[0], seg_send.at[1], seg_recv.at[1], d, (s + 2) % 4)

    @pl.when(s < 3)
    def _():
        seg1.start()

    @pl.when(s < 2)
    def _():
        seg2.start()

    send_kv(0)
    send_kv(1)
    ogs = remote(
        og_hbm.at[:, other], og2.at[pl.ds(toks, toks)], ogs_send, ogs_recv, d, sib
    )
    ogs.start()

    og_copy.wait()
    w_copy.wait()

    def grad_pair(i, c):
        at = pl.ds(pl.multiple_of(i * 2 * HEAD, 2 * HEAD), 2 * HEAD)
        g = dot(w[at, :], og[...], 1, 1).astype(BF16)
        dgrad[2 * i] = g[:HEAD]
        dgrad[2 * i + 1] = g[HEAD:]
        return c

    lax.fori_loop(0, heads // 2, grad_pair, 0)

    @pl.when(s >= 1)
    def _():
        seg1.wait_recv()

    @pl.when(s >= 2)
    def _():
        seg2.wait_recv()

    down = lax.broadcasted_iota(jnp.int32, (toks, toks), 0)
    across = lax.broadcasted_iota(jnp.int32, (toks, toks), 1)
    row = seg_all[2][0:1, :]
    for j in range(3):
        column = jnp.sum(
            jnp.where(down == across, jnp.broadcast_to(seg_all[j][0:1, :], (toks, toks)), 0.0),
            axis=1, keepdims=True,
        )
        seen = column == row
        if j == 2:
            seen = seen & (down <= across)
        bias[j * toks:(j + 1) * toks, :] = jnp.where(seen, 0.0, -1e30)

    pltpu.make_async_copy(q_s, q_s, q_sem).wait()

    def attend(h):
        q = q_s[h]
        k3 = kv[h, :, 0].reshape(3 * toks, HEAD)
        v3 = kv[h, :, 1].reshape(3 * toks, HEAD)
        g = dgrad[h]
        score = dot(k3, q, 1, 1) * (HEAD ** -0.5 * LOG2E) + bias[...]
        raised = jnp.exp2(score - jnp.max(score, axis=0, keepdims=True))
        prob = raised * (1.0 / jnp.sum(raised, axis=0, keepdims=True))
        low = prob.astype(BF16)
        a = dot(v3, low, 0, 0).astype(BF16)
        att[h, :, 0:toks] = a
        delta = jnp.sum(g.astype(F32) * a.astype(F32), axis=0, keepdims=True)
        change = (prob * (dot(v3, g, 1, 0) - delta)).astype(BF16)
        dq = dot(k3, change, 0, 0) * HEAD ** -0.5
        dq_out[:, lanes(h)] = dq.T.astype(BF16)
        dk = dot(change, q, 1, 0) * HEAD ** -0.5
        dv = dot(low, g, 1, 1)
        for i, term in enumerate((dk, dv)):
            dkv_own[h, i] = term[2 * toks:]
            dkv_out[h, 0, i] = term[toks:2 * toks].astype(BF16)
            dkv_out[h, 1, i] = term[:toks].astype(BF16)

    def att_copy(h):
        return remote(
            att.at[h, :, pl.ds(0, toks)], att.at[h, :, pl.ds(toks, toks)],
            att_send.at[h], att_recv.at[h], d, sib,
        )

    def back1(h):
        return remote(
            dkv_out.at[h, 0], dkv_in.at[0, h], dk1_send.at[h], dk1_recv.at[h], d, (s + 3) % 4
        )

    def back2(h):
        return remote(
            dkv_out.at[h, 1], dkv_in.at[1, h], dk2_send.at[h], dk2_recv.at[h], d,
            (s + 3 - (1 - core)) % 4,
        )

    def y1_copy(h, j):
        block = ya if j == 0 else yc
        return remote(
            part.at[h, pl.ds(pl.multiple_of(block * rows, rows), rows)], y1_in.at[h, j],
            y1_send.at[h, j], y1_recv.at[h, j], place(z, ya, hi), s,
        )

    def y2_copy(h):
        return remote(
            y1_sum.at[h], y2_in.at[h], y2_send.at[h], y2_recv.at[h], place(z, yb, hi), s
        )

    def z_copy(t):
        h = (z + 1 + t) % heads
        slot = heads - 2 - t
        return remote(
            z_out.at[h], z_in.at[slot], z_send.at[slot], z_recv.at[slot], place(h, y, hi), s
        )

    def own(h, block):
        return part[h, pl.ds(pl.multiple_of(block * rows, rows), rows), :].astype(F32)

    def step(t, c):
        @pl.when(t < heads - 2)
        def _():
            h = (z + 1 + t) % heads

            @pl.when(s < 3)
            def _():
                kv1(h).wait_send()

            @pl.when(s == 0)
            def _():
                kv2(h).wait_send()

            send_kv(t + 2)

        @pl.when((t >= 1) & (t <= heads))
        def _():
            h = (z + t) % heads

            @pl.when(s == 2)
            def _():
                back2(h).wait_recv()
                dkv_out[h, 0] = (
                    dkv_out[h, 0].astype(F32) + dkv_in[1, h].astype(F32)
                ).astype(BF16)
                back1(h).start()

            att_copy(h).wait_recv()
            part[h] = dot(att[h], og2[...], 1, 0).astype(BF16)
            y1_copy(h, 0).start()
            y1_copy(h, 1).start()

        @pl.when((t >= 2) & (t <= heads + 1))
        def _():
            h = (z + t - 1) % heads
            y1_copy(h, 0).wait_recv()
            y1_copy(h, 1).wait_recv()
            y1_sum[h] = (own(h, yb) + y1_in[h, 1].astype(F32)).astype(BF16)
            y2_copy(h).start()

        @pl.when(t >= 3)
        def _():
            h = (z + t - 2) % heads
            y2_copy(h).wait_recv()
            z_out[h] = (own(h, y) + y1_in[h, 0].astype(F32) + y2_in[h].astype(F32)).astype(BF16)

            @pl.when(t < heads + 2)
            def _():
                z_copy(t - 3).start()

        @pl.when(t < heads)
        def _():
            h = (z + 1 + t) % heads

            @pl.when(s >= 1)
            def _():
                kv1(h).wait_recv()

            @pl.when(s == 2)
            def _():
                kv2_relay(h).start()

            @pl.when(s >= 2)
            def _():
                kv2(h).wait_recv()

            attend(h)
            att_copy(h).start()

            @pl.when((s == 1) | (s == 3))
            def _():
                back1(h).start()

            @pl.when(s >= 2)
            def _():
                back2(h).start()

        @pl.when(t == heads)
        def _():
            flat = att[:, :, 0:toks].reshape(heads * HEAD, toks).T

            def project(i, cc):
                at = pl.ds(pl.multiple_of(i * 512, 512), 512)
                proj_out[:, at] = dot(flat, w[:, at], 1, 0).astype(BF16)
                return cc

            width = proj_out.shape[1]
            if width >= 512:
                lax.fori_loop(0, width // 512, project, 0)
            else:
                proj_out[...] = dot(flat, w[...], 1, 0).astype(BF16)

        return c

    og2_copy.wait()
    ogs.wait_recv()
    lax.fori_loop(0, heads + 3, step, 0)

    total = z_out[z].astype(F32)
    for slot in range(PLANES - 1):
        z_copy(heads - 2 - slot).wait_recv()
        total = total + z_in[slot].astype(F32)
    x_out[...] = total
    x_copies = []
    targets = [(d, (1 - lo) * 2 + core, hi)]
    if SIDES == 2:
        targets += [(place(z, y, 1 - hi), core, 1 - hi), (place(z, y, 1 - hi), 2 + core, 1 - hi)]
    for i, (dp, seq, part_of) in enumerate(targets):
        slot = i if i == 0 else 1 + (i - 1 + lo) % 2
        copy = remote(
            x_out.at[pl.ds(pl.multiple_of(part_of * share, share), share)], x_in.at[slot],
            x_send.at[i], x_recv.at[slot], dp, seq,
        )
        copy.start()
        x_copies.append(copy)

    def finish(h, c):
        @pl.when(s < 3)
        def _():
            back1(h).wait_recv()

        @pl.when(s == 0)
        def _():
            back2(h).wait_recv()

        for i, out in enumerate((dk_out, dv_out)):
            @pl.when(s == 3)
            def _():
                out[:, lanes(h)] = dkv_own[h, i].astype(BF16)

            @pl.when((s == 1) | (s == 2))
            def _():
                out[:, lanes(h)] = (dkv_own[h, i] + dkv_in[0, h, i].astype(F32)).astype(BF16)

            @pl.when(s == 0)
            def _():
                out[:, lanes(h)] = (
                    dkv_own[h, i] + dkv_in[0, h, i].astype(F32) + dkv_in[1, h, i].astype(F32)
                ).astype(BF16)

        return c

    lax.fori_loop(0, heads, finish, 0)

    result = x_out[pl.ds(pl.multiple_of(hi * share, share), share), :]
    for slot in range(len(targets)):
        pltpu.make_async_copy(x_in.at[slot], x_in.at[slot], x_recv.at[slot]).wait()
        result = result + x_in[slot]
    fin[...] = result.astype(BF16)
    last = remote(fin, fin_in, f_send, f_recv, d, sib)
    last.start()
    wg_out[:, mine] = fin[...]

    def drain(h, c):
        @pl.when((s < 3) & (h >= heads - 2))
        def _():
            kv1((z + 1 + h) % heads).wait_send()

        @pl.when((s == 0) & (h >= heads - 2))
        def _():
            kv2((z + 1 + h) % heads).wait_send()

        @pl.when(s == 2)
        def _():
            kv2_relay(h).wait_send()

        @pl.when(s >= 1)
        def _():
            back1(h).wait_send()

        @pl.when(s >= 2)
        def _():
            back2(h).wait_send()

        att_copy(h).wait_send()
        y1_copy(h, 0).wait_send()
        y1_copy(h, 1).wait_send()
        y2_copy(h).wait_send()

        @pl.when(h < heads - 1)
        def _():
            z_copy(h).wait_send()

        return c

    lax.fori_loop(0, heads, drain, 0)
    ogs.wait_send()
    for copy in x_copies:
        copy.wait_send()

    @pl.when(s < 3)
    def _():
        seg1.wait_send()

    @pl.when(s < 2)
    def _():
        seg2.wait_send()

    last.wait()
    wg_out[:, other] = fin_in[...]


def body(queries, keys, values, segment_ids, out_weight, out_grad):
    toks, hd = queries.shape[1:]
    width = out_grad.shape[2]
    heads = hd // HEAD
    cols = width // 2
    rows = HEAD // RING
    share = rows // SIDES
    sem = pltpu.SemaphoreType.DMA
    any_space = pl.BlockSpec(memory_space=pl.ANY)
    in_vmem = pl.BlockSpec(memory_space=pltpu.VMEM)
    outs = pl.pallas_call(
        kernel,
        out_shape=(
            jax.ShapeDtypeStruct((toks, width), BF16),
            jax.ShapeDtypeStruct((toks, hd), BF16),
            jax.ShapeDtypeStruct((toks, hd), BF16),
            jax.ShapeDtypeStruct((toks, hd), BF16),
            jax.ShapeDtypeStruct((share, width), BF16),
        ),
        in_specs=[any_space, any_space, any_space, in_vmem, any_space, any_space],
        out_specs=(in_vmem,) * 5,
        scratch_shapes=[
            pltpu.VMEM((heads, toks, HEAD), BF16),
            pltpu.VMEM((heads, 3, 2, toks, HEAD), BF16),
            pltpu.VMEM((toks, width), BF16),
            pltpu.VMEM((hd, width), BF16),
            pltpu.VMEM((2 * toks, cols), BF16),
            pltpu.VMEM((heads, HEAD, toks), BF16),
            pltpu.VMEM((heads, HEAD, 2 * toks), BF16),
            pltpu.VMEM((8, toks), F32),
            pltpu.VMEM((3, 8, toks), F32),
            pltpu.VMEM((3 * toks, toks), F32),
            pltpu.VMEM((heads, 2, toks, HEAD), F32),
            pltpu.VMEM((heads, 2, 2, toks, HEAD), BF16),
            pltpu.VMEM((2, heads, 2, toks, HEAD), BF16),
            pltpu.VMEM((heads, HEAD, cols), BF16),
            pltpu.VMEM((heads, 2, rows, cols), BF16),
            pltpu.VMEM((heads, rows, cols), BF16),
            pltpu.VMEM((heads, rows, cols), BF16),
            pltpu.VMEM((heads, rows, cols), BF16),
            pltpu.VMEM((PLANES - 1, rows, cols), BF16),
            pltpu.VMEM((rows, cols), F32),
            pltpu.VMEM((3, share, cols), F32),
            pltpu.VMEM((share, cols), BF16),
            pltpu.VMEM((share, cols), BF16),
            sem, sem((heads,)), sem, sem, sem, sem((2,)), sem((2,)), sem, sem,
            sem((heads,)), sem((heads,)), sem((heads,)), sem((heads,)),
            sem((heads,)), sem((heads,)), sem((heads,)), sem((heads,)),
            sem((heads,)), sem((heads,)), sem((heads, 2)), sem((heads, 2)),
            sem((heads,)), sem((heads,)), sem((PLANES - 1,)), sem((PLANES - 1,)),
            sem((3,)), sem((3,)), sem, sem,
        ],
        compiler_params=pltpu.CompilerParams(
            collective_id=0, has_side_effects=True, vmem_limit_bytes=56 << 20
        ),
        cost_estimate=pl.CostEstimate(
            flops=8 << 30, bytes_accessed=10 << 20, transcendentals=2 << 20
        ),
    )(queries[0], keys[0], values[0], segment_ids, out_weight, out_grad[0])
    return tuple(out[None] for out in outs[:4]) + (outs[4],)


def solution(mesh):
    placed = (
        P("dp", "seq", None),
        P("dp", "seq", None),
        P("dp", "seq", None),
        P("dp", "seq"),
        P(),
        P("dp", "seq", None),
    )
    return jax.shard_map(
        body,
        mesh=mesh,
        in_specs=placed,
        out_specs=placed[:1] * 4 + (P("dp", None),),
        check_vma=False,
    )
```

```python
import jax
import jax.numpy as jnp
from jax import lax
from jax.experimental import pallas as pl
from jax.experimental.pallas import tpu as pltpu
from jax.sharding import PartitionSpec as P

HEAD = 128
PLANES, RING, SIDES = 8, 4, 2
AHEAD = 2
MESH = pl.DeviceIdType.MESH
F32, BF16 = jnp.float32, jnp.bfloat16
LOG2E = 1.4426950408889634


def dot(a, b, ca, cb):
    return lax.dot_general(a, b, (((ca,), (cb,)), ((), ())), preferred_element_type=F32)


def kernel(
    q_hbm, k_hbm, v_hbm, seg_ref, w_hbm, og_hbm,
    proj_out, dq_out, dk_out, dv_out, wg_out,
    q_s, kv, og, w, og2, dgrad, att, seg_own, seg_all, bias,
    dkv_own, dkv_out, dkv_in, part, y1_in, y1_sum, y2_in, z_out, z_in, x_out, x_in, fin, fin_in,
    q_sem, kv_sem, og_sem, w_sem, og2_sem, seg_send, seg_recv, ogs_send, ogs_recv,
    kv1_send, kv1_recv, kv2_send, kv2_recv, dk1_send, dk1_recv, dk2_send, dk2_recv,
    att_send, att_recv, y1_send, y1_recv, y2_send, y2_recv, z_send, z_recv,
    x_send, x_recv, f_send, f_recv,
):
    heads, toks = q_s.shape[0], q_s.shape[1]
    cols = og2.shape[1]
    rows = HEAD // RING
    share = rows // SIDES
    s = lax.axis_index("seq")
    d = lax.axis_index("dp")
    core = s % 2
    lo = s // 2
    z = d // (RING * SIDES)
    y = (d // SIDES) % RING
    hi = d % SIDES
    sib = s + 1 - 2 * core
    flip = y + 1 - 2 * (y % 2)
    mirror = RING - 1 - y
    ya = core * mirror + (1 - core) * flip
    yb = core * flip + (1 - core) * mirror
    yc = (y + 2) % RING

    def place(zz, yy, xx):
        return zz * (RING * SIDES) + yy * SIDES + xx

    def remote(src, dst, send, recv, dp, seq):
        return pltpu.make_async_remote_copy(
            src_ref=src, dst_ref=dst, send_sem=send, recv_sem=recv,
            device_id=(dp, seq), device_id_type=MESH,
        )

    def lanes(h):
        return pl.ds(pl.multiple_of(h * HEAD, HEAD), HEAD)

    def apart(t):
        even = heads // 2 + t // 2
        odd = (heads - 1 - t) // 2
        return even + (t % 2) * (odd - even)

    def order(t):
        return (z + apart(t)) % heads

    def load_head(i, c):
        h = order(i)
        pltpu.make_async_copy(k_hbm.at[:, lanes(h)], kv.at[h, 2, 0], kv_sem.at[h]).start()
        pltpu.make_async_copy(v_hbm.at[:, lanes(h)], kv.at[h, 2, 1], kv_sem.at[h]).start()
        return c

    lax.fori_loop(0, heads, load_head, 0)
    og_copy = pltpu.make_async_copy(og_hbm, og, og_sem)
    w_copy = pltpu.make_async_copy(w_hbm, w, w_sem)
    og_copy.start()
    w_copy.start()

    def load_query(i, c):
        pltpu.make_async_copy(q_hbm.at[:, lanes(i)], q_s.at[i], q_sem).start()
        return c

    lax.fori_loop(0, heads, load_query, 0)
    mine = pl.ds(pl.multiple_of(core * cols, cols), cols)
    other = pl.ds(pl.multiple_of((1 - core) * cols, cols), cols)
    og2_copy = pltpu.make_async_copy(og_hbm.at[:, mine], og2.at[pl.ds(0, toks)], og2_sem)
    og2_copy.start()

    barrier = pltpu.get_barrier_semaphore()
    peers = [(d, (s + 1) % 4), (d, (s + 2) % 4), (d, (s + 3) % 4)]
    peers += [(place(z, flip, hi), s), (place(z, mirror, hi), s)]
    peers += [(place((z + i) % PLANES, y, hi), s) for i in range(1, PLANES)]
    if SIDES == 2:
        peers += [(place(z, y, 1 - hi), core), (place(z, y, 1 - hi), 2 + core)]
    for peer in peers:
        pl.semaphore_signal(barrier, inc=1, device_id=peer, device_id_type=MESH)

    seg_own[...] = jnp.broadcast_to(seg_ref[0:1, :].astype(F32), seg_own.shape)
    seg_all[2] = seg_own[...]

    @pl.when(s < 2)
    def _():
        seg_all[0] = jnp.full(seg_own.shape, -1.0, F32)

        def clear(h, c):
            kv[h, 0] = jnp.zeros((2, toks, HEAD), BF16)
            return c

        lax.fori_loop(0, heads, clear, 0)

    @pl.when(s < 1)
    def _():
        seg_all[1] = jnp.full(seg_own.shape, -1.0, F32)

        def clear(h, c):
            kv[h, 1] = jnp.zeros((2, toks, HEAD), BF16)
            return c

        lax.fori_loop(0, heads, clear, 0)

    def wait_head(h, c):
        pltpu.make_async_copy(kv.at[h, 2], kv.at[h, 2], kv_sem.at[h]).wait()
        return c

    lax.fori_loop(0, heads, wait_head, 0)
    pl.semaphore_wait(barrier, len(peers))

    def kv1(h):
        return remote(kv.at[h, 2], kv.at[h, 1], kv1_send.at[h], kv1_recv.at[h], d, (s + 1) % 4)

    def kv2(h):
        return remote(kv.at[h, 2], kv.at[h, 0], kv2_send.at[h], kv2_recv.at[h], d, (s + 2) % 4)

    def kv2_relay(h):
        return remote(kv.at[h, 1], kv.at[h, 0], kv2_send.at[h], kv2_recv.at[h], d, (s + 1) % 4)

    def send_kv(t):
        h = order(t)

        @pl.when(s < 3)
        def _():
            kv1(h).start()

        @pl.when(s == 0)
        def _():
            kv2(h).start()

    seg1 = remote(seg_own, seg_all.at[1], seg_send.at[0], seg_recv.at[0], d, (s + 1) % 4)
    seg2 = remote(seg_own, seg_all.at[0], seg_send.at[1], seg_recv.at[1], d, (s + 2) % 4)

    @pl.when(s < 3)
    def _():
        seg1.start()

    @pl.when(s < 2)
    def _():
        seg2.start()

    send_kv(0)
    og_copy.wait()
    ogs = remote(
        og.at[:, other], og2.at[pl.ds(toks, toks)], ogs_send, ogs_recv, d, sib
    )
    ogs.start()
    w_copy.wait()

    def grad_pair(i, c):
        at = pl.ds(pl.multiple_of(i * 2 * HEAD, 2 * HEAD), 2 * HEAD)
        g = dot(w[at, :], og[...], 1, 1).astype(BF16)
        dgrad[2 * i] = g[:HEAD]
        dgrad[2 * i + 1] = g[HEAD:]
        return c

    lax.fori_loop(0, heads // 2, grad_pair, 0)
    for t in range(1, AHEAD):
        send_kv(t)

    @pl.when(s >= 1)
    def _():
        seg1.wait_recv()

    @pl.when(s >= 2)
    def _():
        seg2.wait_recv()

    down = lax.broadcasted_iota(jnp.int32, (toks, toks), 0)
    across = lax.broadcasted_iota(jnp.int32, (toks, toks), 1)
    row = seg_all[2][0:1, :]
    for j in range(3):
        column = jnp.sum(
            jnp.where(down == across, jnp.broadcast_to(seg_all[j][0:1, :], (toks, toks)), 0.0),
            axis=1, keepdims=True,
        )
        seen = column == row
        if j == 2:
            seen = seen & (down <= across)
        bias[j * toks:(j + 1) * toks, :] = jnp.where(seen, 0.0, -1e30)

    pltpu.make_async_copy(q_s, q_s, q_sem).wait()

    def attend(h):
        q = q_s[h]
        k3 = kv[h, :, 0].reshape(3 * toks, HEAD)
        v3 = kv[h, :, 1].reshape(3 * toks, HEAD)
        g = dgrad[h]
        score = dot(k3, q, 1, 1) * (HEAD ** -0.5 * LOG2E) + bias[...]
        raised = jnp.exp2(score - jnp.max(score, axis=0, keepdims=True))
        prob = raised * (1.0 / jnp.sum(raised, axis=0, keepdims=True))
        low = prob.astype(BF16)
        a = dot(v3, low, 0, 0).astype(BF16)
        att[h, :, 0:toks] = a
        att_copy(h).start()
        delta = jnp.sum(g.astype(F32) * a.astype(F32), axis=0, keepdims=True)
        change = (prob * (dot(v3, g, 1, 0) - delta)).astype(BF16)
        dq = dot(k3, change, 0, 0) * HEAD ** -0.5
        dq_out[:, lanes(h)] = dq.T.astype(BF16)
        dk = dot(change, q, 1, 0) * HEAD ** -0.5
        dv = dot(low, g, 1, 1)
        for i, term in enumerate((dk, dv)):
            dkv_own[h, i] = term[2 * toks:]
            dkv_out[h, 0, i] = term[toks:2 * toks].astype(BF16)
            dkv_out[h, 1, i] = term[:toks].astype(BF16)

    def att_copy(h):
        return remote(
            att.at[h, :, pl.ds(0, toks)], att.at[h, :, pl.ds(toks, toks)],
            att_send.at[h], att_recv.at[h], d, sib,
        )

    def back1(h):
        return remote(
            dkv_out.at[h, 0], dkv_in.at[0, h], dk1_send.at[h], dk1_recv.at[h], d, (s + 3) % 4
        )

    def back2(h):
        return remote(
            dkv_out.at[h, 1], dkv_in.at[1, h], dk2_send.at[h], dk2_recv.at[h], d,
            (s + 3 - (1 - core)) % 4,
        )

    def y1_copy(h, j):
        block = ya if j == 0 else yc
        return remote(
            part.at[h, pl.ds(pl.multiple_of(block * rows, rows), rows)], y1_in.at[h, j],
            y1_send.at[h, j], y1_recv.at[h, j], place(z, ya, hi), s,
        )

    def y2_copy(h):
        return remote(
            y1_sum.at[h], y2_in.at[h], y2_send.at[h], y2_recv.at[h], place(z, yb, hi), s
        )

    def z_copy(t):
        h = order(t)
        slot = heads - 1 - apart(t)
        return remote(
            z_out.at[h], z_in.at[slot], z_send.at[slot], z_recv.at[slot], place(h, y, hi), s
        )

    def own(h, block):
        return part[h, pl.ds(pl.multiple_of(block * rows, rows), rows), :].astype(F32)

    def step(t, c):
        @pl.when((t < heads) & (s >= 1))
        def _():
            h = order(t)
            kv1(h).wait_recv()

            @pl.when(s == 2)
            def _():
                kv2_relay(h).start()

        @pl.when(t < heads)
        def _():
            h = order(t)

            @pl.when(s >= 2)
            def _():
                kv2(h).wait_recv()

            attend(h)

            @pl.when((s == 1) | (s == 3))
            def _():
                back1(h).start()

            @pl.when(s >= 2)
            def _():
                back2(h).start()

        @pl.when((t >= 1) & (t <= heads))
        def _():
            h = order(t - 1)
            att_copy(h).wait_recv()
            part[h] = dot(att[h], og2[...], 1, 0).astype(BF16)
            y1_copy(h, 0).start()
            y1_copy(h, 1).start()

        @pl.when((s == 2) & (t >= 1) & (t <= heads))
        def _():
            h = order(t - 1)
            back2(h).wait_recv()
            dkv_out[h, 0] = (
                dkv_out[h, 0].astype(F32) + dkv_in[1, h].astype(F32)
            ).astype(BF16)
            back1(h).start()

        @pl.when(t < heads - AHEAD)
        def _():
            h = order(t)

            @pl.when(s < 3)
            def _():
                kv1(h).wait_send()

            @pl.when(s == 0)
            def _():
                kv2(h).wait_send()

            send_kv(t + AHEAD)

        @pl.when(t == heads)
        def _():
            flat = att[:, :, 0:toks].reshape(heads * HEAD, toks).T

            def project(i, cc):
                at = pl.ds(pl.multiple_of(i * 512, 512), 512)
                proj_out[:, at] = dot(flat, w[:, at], 1, 0).astype(BF16)
                return cc

            width = proj_out.shape[1]
            if width >= 512:
                lax.fori_loop(0, width // 512, project, 0)
            else:
                proj_out[...] = dot(flat, w[...], 1, 0).astype(BF16)

        @pl.when((t >= 3) & (t <= heads + 2))
        def _():
            h = order(t - 3)
            y1_copy(h, 0).wait_recv()
            y1_copy(h, 1).wait_recv()
            y1_sum[h] = (own(h, yb) + y1_in[h, 1].astype(F32)).astype(BF16)
            y2_copy(h).start()

        @pl.when(t >= 5)
        def _():
            h = order(t - 5)
            y2_copy(h).wait_recv()
            z_out[h] = (own(h, y) + y1_in[h, 0].astype(F32) + y2_in[h].astype(F32)).astype(BF16)

            @pl.when(t < heads + 4)
            def _():
                z_copy(t - 5).start()

        return c

    og2_copy.wait()
    ogs.wait_recv()
    lax.fori_loop(0, heads + 5, step, 0)

    total = z_out[z].astype(F32)
    for t in range(PLANES - 1):
        z_copy(t).wait_recv()
    for slot in range(PLANES - 1):
        total = total + z_in[slot].astype(F32)
    x_out[...] = total.astype(BF16)
    x_copies = []
    targets = [(d, (1 - lo) * 2 + core, hi)]
    if SIDES == 2:
        targets += [(place(z, y, 1 - hi), core, 1 - hi), (place(z, y, 1 - hi), 2 + core, 1 - hi)]
    for i, (dp, seq, part_of) in enumerate(targets):
        slot = i if i == 0 else 1 + (i - 1 + lo) % 2
        copy = remote(
            x_out.at[pl.ds(pl.multiple_of(part_of * share, share), share)], x_in.at[slot],
            x_send.at[i], x_recv.at[slot], dp, seq,
        )
        copy.start()
        x_copies.append(copy)

    def finish(h, c):
        @pl.when(s < 3)
        def _():
            back1(h).wait_recv()

        @pl.when(s == 0)
        def _():
            back2(h).wait_recv()

        for i, out in enumerate((dk_out, dv_out)):
            @pl.when(s == 3)
            def _():
                out[:, lanes(h)] = dkv_own[h, i].astype(BF16)

            @pl.when((s == 1) | (s == 2))
            def _():
                out[:, lanes(h)] = (dkv_own[h, i] + dkv_in[0, h, i].astype(F32)).astype(BF16)

            @pl.when(s == 0)
            def _():
                out[:, lanes(h)] = (
                    dkv_own[h, i] + dkv_in[0, h, i].astype(F32) + dkv_in[1, h, i].astype(F32)
                ).astype(BF16)

        return c

    lax.fori_loop(0, heads, finish, 0)

    result = x_out[pl.ds(pl.multiple_of(hi * share, share), share), :].astype(F32)
    for slot in range(len(targets)):
        pltpu.make_async_copy(x_in.at[slot], x_in.at[slot], x_recv.at[slot]).wait()
        result = result + x_in[slot].astype(F32)
    fin[...] = result.astype(BF16)
    last = remote(fin, fin_in, f_send, f_recv, d, sib)
    last.start()
    wg_out[:, mine] = fin[...]

    def drain(h, c):
        @pl.when((s < 3) & (h >= heads - AHEAD))
        def _():
            kv1(order(h)).wait_send()

        @pl.when((s == 0) & (h >= heads - AHEAD))
        def _():
            kv2(order(h)).wait_send()

        @pl.when(s == 2)
        def _():
            kv2_relay(h).wait_send()

        @pl.when(s >= 1)
        def _():
            back1(h).wait_send()

        @pl.when(s >= 2)
        def _():
            back2(h).wait_send()

        att_copy(h).wait_send()
        y1_copy(h, 0).wait_send()
        y1_copy(h, 1).wait_send()
        y2_copy(h).wait_send()

        @pl.when(h < heads - 1)
        def _():
            z_copy(h).wait_send()

        return c

    lax.fori_loop(0, heads, drain, 0)
    ogs.wait_send()
    for copy in x_copies:
        copy.wait_send()

    @pl.when(s < 3)
    def _():
        seg1.wait_send()

    @pl.when(s < 2)
    def _():
        seg2.wait_send()

    last.wait()
    wg_out[:, other] = fin_in[...]


def settle(*refs):
    count = len(refs) // 2
    copies = [
        pltpu.make_async_copy(src, dst, refs[-1].at[i])
        for i, (src, dst) in enumerate(zip(refs[:count], refs[count:-1]))
    ]
    for copy in copies:
        copy.start()
    for copy in copies:
        copy.wait()


def body(queries, keys, values, segment_ids, out_weight, out_grad):
    toks, hd = queries.shape[1:]
    width = out_grad.shape[2]
    heads = hd // HEAD
    cols = width // 2
    rows = HEAD // RING
    share = rows // SIDES
    sem = pltpu.SemaphoreType.DMA
    any_space = pl.BlockSpec(memory_space=pl.ANY)
    in_vmem = pl.BlockSpec(memory_space=pltpu.VMEM)
    in_hbm = pl.BlockSpec(memory_space=pltpu.HBM)

    def stay(x):
        return pltpu.with_memory_space_constraint(x, pltpu.HBM)

    outs = pl.pallas_call(
        kernel,
        out_shape=(
            pltpu.VMEM((toks, width), BF16),
            pltpu.VMEM((toks, hd), BF16),
            pltpu.VMEM((toks, hd), BF16),
            pltpu.VMEM((toks, hd), BF16),
            pltpu.VMEM((share, width), BF16),
        ),
        in_specs=[in_hbm, in_hbm, in_hbm, in_vmem, in_hbm, in_hbm],
        out_specs=(in_vmem,) * 5,
        scratch_shapes=[
            pltpu.VMEM((heads, toks, HEAD), BF16),
            pltpu.VMEM((heads, 3, 2, toks, HEAD), BF16),
            pltpu.VMEM((toks, width), BF16),
            pltpu.VMEM((hd, width), BF16),
            pltpu.VMEM((2 * toks, cols), BF16),
            pltpu.VMEM((heads, HEAD, toks), BF16),
            pltpu.VMEM((heads, HEAD, 2 * toks), BF16),
            pltpu.VMEM((8, toks), F32),
            pltpu.VMEM((3, 8, toks), F32),
            pltpu.VMEM((3 * toks, toks), F32),
            pltpu.VMEM((heads, 2, toks, HEAD), F32),
            pltpu.VMEM((heads, 2, 2, toks, HEAD), BF16),
            pltpu.VMEM((2, heads, 2, toks, HEAD), BF16),
            pltpu.VMEM((heads, HEAD, cols), BF16),
            pltpu.VMEM((heads, 2, rows, cols), BF16),
            pltpu.VMEM((heads, rows, cols), BF16),
            pltpu.VMEM((heads, rows, cols), BF16),
            pltpu.VMEM((heads, rows, cols), BF16),
            pltpu.VMEM((PLANES - 1, rows, cols), BF16),
            pltpu.VMEM((rows, cols), BF16),
            pltpu.VMEM((3, share, cols), BF16),
            pltpu.VMEM((share, cols), BF16),
            pltpu.VMEM((share, cols), BF16),
            sem, sem((heads,)), sem, sem, sem, sem((2,)), sem((2,)), sem, sem,
            sem((heads,)), sem((heads,)), sem((heads,)), sem((heads,)),
            sem((heads,)), sem((heads,)), sem((heads,)), sem((heads,)),
            sem((heads,)), sem((heads,)), sem((heads, 2)), sem((heads, 2)),
            sem((heads,)), sem((heads,)), sem((PLANES - 1,)), sem((PLANES - 1,)),
            sem((3,)), sem((3,)), sem, sem,
        ],
        compiler_params=pltpu.CompilerParams(
            collective_id=0, has_side_effects=True, vmem_limit_bytes=54 << 20
        ),
        cost_estimate=pl.CostEstimate(
            flops=8 << 30, bytes_accessed=10 << 20, transcendentals=2 << 20
        ),
    )(
        stay(queries[0]), stay(keys[0]), stay(values[0]), segment_ids, stay(out_weight),
        stay(out_grad[0]),
    )
    outs = pl.pallas_call(
        settle,
        out_shape=tuple(jax.ShapeDtypeStruct(out.shape, out.dtype) for out in outs),
        in_specs=[in_vmem] * 5,
        out_specs=(any_space,) * 5,
        scratch_shapes=[sem((5,))],
        compiler_params=pltpu.CompilerParams(vmem_limit_bytes=4 << 20),
    )(*[pltpu.with_memory_space_constraint(out, pltpu.VMEM) for out in outs])
    return tuple(out[None] for out in outs[:4]) + (outs[4],)


def solution(mesh):
    placed = (
        P("dp", "seq", None),
        P("dp", "seq", None),
        P("dp", "seq", None),
        P("dp", "seq"),
        P(),
        P("dp", "seq", None),
    )
    return jax.shard_map(
        body,
        mesh=mesh,
        in_specs=placed,
        out_specs=placed[:1] * 4 + (P("dp", None),),
        check_vma=False,
    )
```

```python
import jax
import jax.numpy as jnp
from jax import lax
from jax.experimental import pallas as pl
from jax.experimental.pallas import tpu as pltpu
from jax.sharding import PartitionSpec as P

HEAD = 128
PLANES, RING, SIDES = 8, 4, 2
AHEAD = 2
LAG = 3
MESH = pl.DeviceIdType.MESH
F32, BF16 = jnp.float32, jnp.bfloat16
LOG2E = 1.4426950408889634


def dot(a, b, ca, cb):
    return lax.dot_general(a, b, (((ca,), (cb,)), ((), ())), preferred_element_type=F32)


def kernel(
    q_hbm, k_hbm, v_hbm, seg_ref, w_hbm, og_hbm,
    proj_out, dq_out, dk_out, dv_out, wg_out,
    q_s, kv, og, w, og2, dgrad, att, seg_own, seg_all, bias,
    dkv_own, dkv_out, dkv_in, part, y_in, z_out, z_in, x_out, x_in, fin, fin_in,
    q_sem, kv_sem, og_sem, w_sem, og2_sem, seg_send, seg_recv, ogs_send, ogs_recv,
    kv1_send, kv1_recv, kv2_send, kv2_recv, dk1_send, dk1_recv, dk2_send, dk2_recv,
    att_send, att_recv, y_send, y_recv, z_send, z_recv,
    x_send, x_recv, f_send, f_recv,
):
    heads, toks = q_s.shape[0], q_s.shape[1]
    cols = og2.shape[1]
    rows = HEAD // RING
    share = rows // SIDES
    s = lax.axis_index("seq")
    d = lax.axis_index("dp")
    core = s % 2
    lo = s // 2
    z = d // (RING * SIDES)
    y = (d // SIDES) % RING
    hi = d % SIDES
    sib = s + 1 - 2 * core
    def place(zz, yy, xx):
        return zz * (RING * SIDES) + yy * SIDES + xx

    def remote(src, dst, send, recv, dp, seq):
        return pltpu.make_async_remote_copy(
            src_ref=src, dst_ref=dst, send_sem=send, recv_sem=recv,
            device_id=(dp, seq), device_id_type=MESH,
        )

    def lanes(h):
        return pl.ds(pl.multiple_of(h * HEAD, HEAD), HEAD)

    def apart(t):
        even = heads // 2 + t // 2
        odd = (heads - 1 - t) // 2
        return even + (t % 2) * (odd - even)

    def order(t):
        return (z + apart(t)) % heads

    barrier = pltpu.get_barrier_semaphore()
    peers = [(d, (s + 1) % 4), (d, (s + 2) % 4), (d, (s + 3) % 4)]
    peers += [(place(z, (y + i) % RING, hi), s) for i in range(1, RING)]
    peers += [(place((z + i) % PLANES, y, hi), s) for i in range(1, PLANES)]
    if SIDES == 2:
        peers += [(place(z, y, 1 - hi), core), (place(z, y, 1 - hi), 2 + core)]
    for peer in peers:
        pl.semaphore_signal(barrier, inc=1, device_id=peer, device_id_type=MESH)

    def load_head(i, c):
        h = order(i)
        pltpu.make_async_copy(k_hbm.at[:, lanes(h)], kv.at[h, 2, 0], kv_sem.at[h]).start()
        pltpu.make_async_copy(v_hbm.at[:, lanes(h)], kv.at[h, 2, 1], kv_sem.at[h]).start()
        return c

    lax.fori_loop(0, heads, load_head, 0)
    og_copy = pltpu.make_async_copy(og_hbm, og, og_sem)
    w_copy = pltpu.make_async_copy(w_hbm, w, w_sem)
    og_copy.start()
    w_copy.start()

    def load_query(i, c):
        pltpu.make_async_copy(q_hbm.at[:, lanes(i)], q_s.at[i], q_sem).start()
        return c

    lax.fori_loop(0, heads, load_query, 0)
    mine = pl.ds(pl.multiple_of(core * cols, cols), cols)
    other = pl.ds(pl.multiple_of((1 - core) * cols, cols), cols)
    og2_copy = pltpu.make_async_copy(og_hbm.at[:, mine], og2.at[pl.ds(0, toks)], og2_sem)
    og2_copy.start()

    seg_own[...] = jnp.broadcast_to(seg_ref[0:1, :].astype(F32), seg_own.shape)
    seg_all[2] = seg_own[...]

    @pl.when(s < 2)
    def _():
        seg_all[0] = jnp.full(seg_own.shape, -1.0, F32)

        def clear(h, c):
            kv[h, 0] = jnp.zeros((2, toks, HEAD), BF16)
            return c

        lax.fori_loop(0, heads, clear, 0)

    @pl.when(s < 1)
    def _():
        seg_all[1] = jnp.full(seg_own.shape, -1.0, F32)

        def clear(h, c):
            kv[h, 1] = jnp.zeros((2, toks, HEAD), BF16)
            return c

        lax.fori_loop(0, heads, clear, 0)

    def wait_head(h, c):
        pltpu.make_async_copy(kv.at[h, 2], kv.at[h, 2], kv_sem.at[h]).wait()
        return c

    lax.fori_loop(0, heads, wait_head, 0)
    pl.semaphore_wait(barrier, len(peers))

    def kv1(h):
        return remote(kv.at[h, 2], kv.at[h, 1], kv1_send.at[h], kv1_recv.at[h], d, (s + 1) % 4)

    def kv2(h):
        return remote(kv.at[h, 2], kv.at[h, 0], kv2_send.at[h], kv2_recv.at[h], d, (s + 2) % 4)

    def kv2_relay(h):
        return remote(kv.at[h, 1], kv.at[h, 0], kv2_send.at[h], kv2_recv.at[h], d, (s + 1) % 4)

    def send_near(t):
        @pl.when(s < 3)
        def _():
            kv1(order(t)).start()

    def send_far(t):
        @pl.when(s == 0)
        def _():
            kv2(order(t)).start()

    send_near(0)
    send_far(0)
    seg1 = remote(seg_own, seg_all.at[1], seg_send.at[0], seg_recv.at[0], d, (s + 1) % 4)
    seg2 = remote(seg_own, seg_all.at[0], seg_send.at[1], seg_recv.at[1], d, (s + 2) % 4)

    @pl.when(s < 3)
    def _():
        seg1.start()

    @pl.when(s < 2)
    def _():
        seg2.start()

    og_copy.wait()
    ogs = remote(
        og.at[:, other], og2.at[pl.ds(toks, toks)], ogs_send, ogs_recv, d, sib
    )
    ogs.start()
    w_copy.wait()

    def grad_pair(i, c):
        at = pl.ds(pl.multiple_of(i * 2 * HEAD, 2 * HEAD), 2 * HEAD)
        g = dot(w[at, :], og[...], 1, 1).astype(BF16)
        dgrad[2 * i] = g[:HEAD]
        dgrad[2 * i + 1] = g[HEAD:]
        return c

    lax.fori_loop(0, heads // 2, grad_pair, 0)
    for t in range(1, AHEAD):
        send_near(t)
        send_far(t)

    @pl.when(s >= 1)
    def _():
        seg1.wait_recv()

    @pl.when(s >= 2)
    def _():
        seg2.wait_recv()

    down = lax.broadcasted_iota(jnp.int32, (toks, toks), 0)
    across = lax.broadcasted_iota(jnp.int32, (toks, toks), 1)
    row = seg_all[2][0:1, :]
    for j in range(3):
        column = jnp.sum(
            jnp.where(down == across, jnp.broadcast_to(seg_all[j][0:1, :], (toks, toks)), 0.0),
            axis=1, keepdims=True,
        )
        seen = column == row
        if j == 2:
            seen = seen & (down <= across)
        bias[j * toks:(j + 1) * toks, :] = jnp.where(seen, 0.0, -1e30)

    pltpu.make_async_copy(q_s, q_s, q_sem).wait()

    def attend(h):
        q = q_s[h]
        k3 = kv[h, :, 0].reshape(3 * toks, HEAD)
        v3 = kv[h, :, 1].reshape(3 * toks, HEAD)
        g = dgrad[h]
        score = dot(k3, q, 1, 1) * (HEAD ** -0.5 * LOG2E) + bias[...]
        raised = jnp.exp2(score - jnp.max(score, axis=0, keepdims=True))
        prob = raised * (1.0 / jnp.sum(raised, axis=0, keepdims=True))
        low = prob.astype(BF16)
        a = dot(v3, low, 0, 0).astype(BF16)
        att[h, :, 0:toks] = a
        att_copy(h).start()
        delta = jnp.sum(g.astype(F32) * a.astype(F32), axis=0, keepdims=True)
        change = (prob * (dot(v3, g, 1, 0) - delta)).astype(BF16)
        dq = dot(k3, change, 0, 0) * HEAD ** -0.5
        dq_out[:, lanes(h)] = dq.T.astype(BF16)
        dk = dot(change, q, 1, 0) * HEAD ** -0.5
        dv = dot(low, g, 1, 1)
        for i, term in enumerate((dk, dv)):
            dkv_own[h, i] = term[2 * toks:]
            dkv_out[h, 0, i] = term[toks:2 * toks].astype(BF16)
            dkv_out[h, 1, i] = term[:toks].astype(BF16)

    def att_copy(h):
        return remote(
            att.at[h, :, pl.ds(0, toks)], att.at[h, :, pl.ds(toks, toks)],
            att_send.at[h], att_recv.at[h], d, sib,
        )

    def back1(h):
        return remote(
            dkv_out.at[h, 0], dkv_in.at[0, h], dk1_send.at[h], dk1_recv.at[h], d, (s + 3) % 4
        )

    def back2(h):
        return remote(
            dkv_out.at[h, 1], dkv_in.at[1, h], dk2_send.at[h], dk2_recv.at[h], d,
            (s + 3 - (1 - core)) % 4,
        )

    def y_copy(h, j):
        to = (y + 1 + j) % RING
        return remote(
            part.at[h, pl.ds(pl.multiple_of(to * rows, rows), rows)], y_in.at[h, j],
            y_send.at[h, j], y_recv.at[h, j], place(z, to, hi), s,
        )

    def z_copy(t):
        h = order(t)
        slot = heads - 1 - apart(t)
        return remote(
            z_out.at[h], z_in.at[slot], z_send.at[slot], z_recv.at[slot], place(h, y, hi), s
        )

    def step(t, c):
        @pl.when((t < heads) & (s >= 1))
        def _():
            h = order(t)
            kv1(h).wait_recv()

            @pl.when(s == 2)
            def _():
                kv2_relay(h).start()

        @pl.when(t < heads)
        def _():
            h = order(t)

            @pl.when(s >= 2)
            def _():
                kv2(h).wait_recv()

            attend(h)

            @pl.when((s == 1) | (s == 3))
            def _():
                back1(h).start()

            @pl.when(s >= 2)
            def _():
                back2(h).start()

        @pl.when((t >= 1) & (t <= heads))
        def _():
            h = order(t - 1)
            att_copy(h).wait_recv()
            part[h] = dot(att[h], og2[...], 1, 0).astype(BF16)
            for j in range(RING - 1):
                y_copy(h, j).start()

        @pl.when((s == 2) & (t >= 2) & (t <= heads + 1))
        def _():
            h = order(t - 2)
            back2(h).wait_recv()
            dkv_out[h, 0] = (
                dkv_out[h, 0].astype(F32) + dkv_in[1, h].astype(F32)
            ).astype(BF16)
            back1(h).start()

        @pl.when(t < heads - AHEAD)
        def _():
            h = order(t)

            @pl.when(s < 3)
            def _():
                kv1(h).wait_send()

            @pl.when(s == 0)
            def _():
                kv2(h).wait_send()

            send_near(t + AHEAD)
            send_far(t + AHEAD)

        @pl.when(t >= LAG)
        def _():
            h = order(t - LAG)
            for j in range(RING - 1):
                y_copy(h, j).wait_recv()
            whole = part[h, pl.ds(pl.multiple_of(y * rows, rows), rows), :].astype(F32)
            for j in range(RING - 1):
                whole = whole + y_in[h, j].astype(F32)
            z_out[h] = whole.astype(BF16)

            @pl.when(t < heads + LAG - 1)
            def _():
                z_copy(t - LAG).start()

        return c

    og2_copy.wait()
    ogs.wait_recv()
    lax.fori_loop(0, heads + LAG, step, 0)

    total = z_out[z].astype(F32)
    for t in range(PLANES - 1):
        z_copy(t).wait_recv()
    for slot in range(PLANES - 1):
        total = total + z_in[slot].astype(F32)
    x_out[...] = total.astype(BF16)
    x_copies = []
    targets = [(d, (1 - lo) * 2 + core, hi)]
    if SIDES == 2:
        targets += [(place(z, y, 1 - hi), core, 1 - hi), (place(z, y, 1 - hi), 2 + core, 1 - hi)]
    for i, (dp, seq, part_of) in enumerate(targets):
        slot = i if i == 0 else 1 + (i - 1 + lo) % 2
        copy = remote(
            x_out.at[pl.ds(pl.multiple_of(part_of * share, share), share)], x_in.at[slot],
            x_send.at[i], x_recv.at[slot], dp, seq,
        )
        copy.start()
        x_copies.append(copy)

    flat = att[:, :, 0:toks].reshape(heads * HEAD, toks).T
    width = proj_out.shape[1]
    span = min(512, width)

    def project(i, c):
        at = pl.ds(pl.multiple_of(i * span, span), span)
        proj_out[:, at] = dot(flat, w[:, at], 1, 0).astype(BF16)
        return c

    lax.fori_loop(0, width // span, project, 0)

    result = x_out[pl.ds(pl.multiple_of(hi * share, share), share), :].astype(F32)
    for slot in range(len(targets)):
        pltpu.make_async_copy(x_in.at[slot], x_in.at[slot], x_recv.at[slot]).wait()
        result = result + x_in[slot].astype(F32)
    fin[...] = result.astype(BF16)
    last = remote(fin, fin_in, f_send, f_recv, d, sib)
    last.start()
    wg_out[:, mine] = fin[...]

    def finish(h, c):
        @pl.when(s < 3)
        def _():
            back1(h).wait_recv()

        @pl.when(s == 0)
        def _():
            back2(h).wait_recv()

        for i, out in enumerate((dk_out, dv_out)):
            @pl.when(s == 3)
            def _():
                out[:, lanes(h)] = dkv_own[h, i].astype(BF16)

            @pl.when((s == 1) | (s == 2))
            def _():
                out[:, lanes(h)] = (dkv_own[h, i] + dkv_in[0, h, i].astype(F32)).astype(BF16)

            @pl.when(s == 0)
            def _():
                out[:, lanes(h)] = (
                    dkv_own[h, i] + dkv_in[0, h, i].astype(F32) + dkv_in[1, h, i].astype(F32)
                ).astype(BF16)

        return c

    lax.fori_loop(0, heads, finish, 0)

    def drain(h, c):
        @pl.when((s < 3) & (h >= heads - AHEAD))
        def _():
            kv1(order(h)).wait_send()

        @pl.when((s == 0) & (h >= heads - AHEAD))
        def _():
            kv2(order(h)).wait_send()

        @pl.when(s == 2)
        def _():
            kv2_relay(h).wait_send()

        @pl.when(s >= 1)
        def _():
            back1(h).wait_send()

        @pl.when(s >= 2)
        def _():
            back2(h).wait_send()

        att_copy(h).wait_send()
        for j in range(RING - 1):
            y_copy(h, j).wait_send()

        @pl.when(h < heads - 1)
        def _():
            z_copy(h).wait_send()

        return c

    lax.fori_loop(0, heads, drain, 0)
    ogs.wait_send()
    for copy in x_copies:
        copy.wait_send()

    @pl.when(s < 3)
    def _():
        seg1.wait_send()

    @pl.when(s < 2)
    def _():
        seg2.wait_send()

    last.wait()
    wg_out[:, other] = fin_in[...]


def settle(*refs):
    count = len(refs) // 2
    copies = [
        pltpu.make_async_copy(src, dst, refs[-1].at[i])
        for i, (src, dst) in enumerate(zip(refs[:count], refs[count:-1]))
    ]
    for copy in copies:
        copy.start()
    for copy in copies:
        copy.wait()


def body(queries, keys, values, segment_ids, out_weight, out_grad):
    toks, hd = queries.shape[1:]
    width = out_grad.shape[2]
    heads = hd // HEAD
    cols = width // 2
    rows = HEAD // RING
    share = rows // SIDES
    sem = pltpu.SemaphoreType.DMA
    any_space = pl.BlockSpec(memory_space=pl.ANY)
    in_vmem = pl.BlockSpec(memory_space=pltpu.VMEM)
    in_hbm = pl.BlockSpec(memory_space=pltpu.HBM)

    def stay(x):
        return pltpu.with_memory_space_constraint(x, pltpu.HBM)

    outs = pl.pallas_call(
        kernel,
        out_shape=(
            pltpu.VMEM((toks, width), BF16),
            pltpu.VMEM((toks, hd), BF16),
            pltpu.VMEM((toks, hd), BF16),
            pltpu.VMEM((toks, hd), BF16),
            pltpu.VMEM((share, width), BF16),
        ),
        in_specs=[in_hbm, in_hbm, in_hbm, in_vmem, in_hbm, in_hbm],
        out_specs=(in_vmem,) * 5,
        scratch_shapes=[
            pltpu.VMEM((heads, toks, HEAD), BF16),
            pltpu.VMEM((heads, 3, 2, toks, HEAD), BF16),
            pltpu.VMEM((toks, width), BF16),
            pltpu.VMEM((hd, width), BF16),
            pltpu.VMEM((2 * toks, cols), BF16),
            pltpu.VMEM((heads, HEAD, toks), BF16),
            pltpu.VMEM((heads, HEAD, 2 * toks), BF16),
            pltpu.VMEM((8, toks), F32),
            pltpu.VMEM((3, 8, toks), F32),
            pltpu.VMEM((3 * toks, toks), F32),
            pltpu.VMEM((heads, 2, toks, HEAD), F32),
            pltpu.VMEM((heads, 2, 2, toks, HEAD), BF16),
            pltpu.VMEM((2, heads, 2, toks, HEAD), BF16),
            pltpu.VMEM((heads, HEAD, cols), BF16),
            pltpu.VMEM((heads, RING - 1, rows, cols), BF16),
            pltpu.VMEM((heads, rows, cols), BF16),
            pltpu.VMEM((PLANES - 1, rows, cols), BF16),
            pltpu.VMEM((rows, cols), BF16),
            pltpu.VMEM((3, share, cols), BF16),
            pltpu.VMEM((share, cols), BF16),
            pltpu.VMEM((share, cols), BF16),
            sem, sem((heads,)), sem, sem, sem, sem((2,)), sem((2,)), sem, sem,
            sem((heads,)), sem((heads,)), sem((heads,)), sem((heads,)),
            sem((heads,)), sem((heads,)), sem((heads,)), sem((heads,)),
            sem((heads,)), sem((heads,)), sem((heads, RING - 1)), sem((heads, RING - 1)),
            sem((PLANES - 1,)), sem((PLANES - 1,)),
            sem((3,)), sem((3,)), sem, sem,
        ],
        compiler_params=pltpu.CompilerParams(
            collective_id=0, has_side_effects=True, vmem_limit_bytes=54 << 20
        ),
        cost_estimate=pl.CostEstimate(
            flops=8 << 30, bytes_accessed=10 << 20, transcendentals=2 << 20
        ),
    )(
        stay(queries[0]), stay(keys[0]), stay(values[0]), segment_ids, stay(out_weight),
        stay(out_grad[0]),
    )
    outs = pl.pallas_call(
        settle,
        out_shape=tuple(jax.ShapeDtypeStruct(out.shape, out.dtype) for out in outs),
        in_specs=[in_vmem] * 5,
        out_specs=(any_space,) * 5,
        scratch_shapes=[sem((5,))],
        compiler_params=pltpu.CompilerParams(vmem_limit_bytes=4 << 20),
    )(*[pltpu.with_memory_space_constraint(out, pltpu.VMEM) for out in outs])
    return tuple(out[None] for out in outs[:4]) + (outs[4],)


def solution(mesh):
    placed = (
        P("dp", "seq", None),
        P("dp", "seq", None),
        P("dp", "seq", None),
        P("dp", "seq"),
        P(),
        P("dp", "seq", None),
    )
    return jax.shard_map(
        body,
        mesh=mesh,
        in_specs=placed,
        out_specs=placed[:1] * 4 + (P("dp", None),),
        check_vma=False,
    )
```

```python
import jax
import jax.numpy as jnp
from jax import lax
from jax.experimental import pallas as pl
from jax.experimental.pallas import tpu as pltpu
from jax.sharding import PartitionSpec as P

HEAD = 128
PLANES, RING, SIDES = 8, 4, 2
AHEAD = 2
LAG = 4
MESH = pl.DeviceIdType.MESH
F32, BF16 = jnp.float32, jnp.bfloat16
LOG2E = 1.4426950408889634


def dot(a, b, ca, cb):
    return lax.dot_general(a, b, (((ca,), (cb,)), ((), ())), preferred_element_type=F32)


def kernel(
    q_hbm, k_hbm, v_hbm, seg_ref, w_hbm, og_hbm,
    proj_out, dq_out, dk_out, dv_out, wg_out,
    q_s, kv, og, w, og2, dgrad, att, seg_own, seg_all, bias,
    dkv_own, dkv_out, dkv_in, part, y_in, z_out, z_in, x_out, x_in,
    q_sem, kv_sem, og_sem, w_sem, og2_sem, seg_send, seg_recv, ogs_send, ogs_recv,
    kv1_send, kv1_recv, kv2_send, kv2_recv, dk1_send, dk1_recv, dk2_send, dk2_recv,
    att_send, att_recv, y_send, y_recv, z_send, z_recv,
    x_send, x_recv,
):
    heads, toks = q_s.shape[0], q_s.shape[1]
    cols = og2.shape[1]
    rows = HEAD // RING
    share = rows // SIDES
    s = lax.axis_index("seq")
    d = lax.axis_index("dp")
    core = s % 2
    lo = s // 2
    z = d // (RING * SIDES)
    y = (d // SIDES) % RING
    hi = d % SIDES
    sib = s + 1 - 2 * core
    def place(zz, yy, xx):
        return zz * (RING * SIDES) + yy * SIDES + xx

    def remote(src, dst, send, recv, dp, seq):
        return pltpu.make_async_remote_copy(
            src_ref=src, dst_ref=dst, send_sem=send, recv_sem=recv,
            device_id=(dp, seq), device_id_type=MESH,
        )

    def lanes(h):
        return pl.ds(pl.multiple_of(h * HEAD, HEAD), HEAD)

    def apart(t):
        even = heads // 2 + t // 2
        odd = (heads - 1 - t) // 2
        return even + (t % 2) * (odd - even)

    def order(t):
        return (z + apart(t)) % heads

    barrier = pltpu.get_barrier_semaphore()
    peers = [(d, (s + 1) % 4), (d, (s + 2) % 4), (d, (s + 3) % 4)]
    peers += [(place(z, (y + i) % RING, hi), s) for i in range(1, RING)]
    peers += [(place((z + i) % PLANES, y, hi), s) for i in range(1, PLANES)]
    peers += [(place(z, y, 1 - hi), i) for i in range(4)]
    for peer in peers:
        pl.semaphore_signal(barrier, inc=1, device_id=peer, device_id_type=MESH)

    def load_head(i, c):
        h = order(i)
        pltpu.make_async_copy(k_hbm.at[:, lanes(h)], kv.at[h, 2, 0], kv_sem.at[h]).start()
        pltpu.make_async_copy(v_hbm.at[:, lanes(h)], kv.at[h, 2, 1], kv_sem.at[h]).start()
        return c

    lax.fori_loop(0, heads, load_head, 0)
    og_copy = pltpu.make_async_copy(og_hbm, og, og_sem)
    w_copy = pltpu.make_async_copy(w_hbm, w, w_sem)
    og_copy.start()
    w_copy.start()

    def load_query(i, c):
        pltpu.make_async_copy(q_hbm.at[:, lanes(i)], q_s.at[i], q_sem).start()
        return c

    lax.fori_loop(0, heads, load_query, 0)
    mine = pl.ds(pl.multiple_of(core * cols, cols), cols)
    other = pl.ds(pl.multiple_of((1 - core) * cols, cols), cols)
    og2_copy = pltpu.make_async_copy(og_hbm.at[:, mine], og2.at[pl.ds(0, toks)], og2_sem)
    og2_copy.start()

    seg_own[...] = jnp.broadcast_to(seg_ref[0:1, :].astype(F32), seg_own.shape)
    seg_all[2] = seg_own[...]

    @pl.when(s < 2)
    def _():
        seg_all[0] = jnp.full(seg_own.shape, -1.0, F32)

        def clear(h, c):
            kv[h, 0] = jnp.zeros((2, toks, HEAD), BF16)
            return c

        lax.fori_loop(0, heads, clear, 0)

    @pl.when(s < 1)
    def _():
        seg_all[1] = jnp.full(seg_own.shape, -1.0, F32)

        def clear(h, c):
            kv[h, 1] = jnp.zeros((2, toks, HEAD), BF16)
            return c

        lax.fori_loop(0, heads, clear, 0)

    def wait_head(h, c):
        pltpu.make_async_copy(kv.at[h, 2], kv.at[h, 2], kv_sem.at[h]).wait()
        return c

    lax.fori_loop(0, heads, wait_head, 0)
    pl.semaphore_wait(barrier, len(peers))

    def kv1(h):
        return remote(kv.at[h, 2], kv.at[h, 1], kv1_send.at[h], kv1_recv.at[h], d, (s + 1) % 4)

    def kv2(h):
        return remote(kv.at[h, 2], kv.at[h, 0], kv2_send.at[h], kv2_recv.at[h], d, (s + 2) % 4)

    def kv2_relay(h):
        return remote(kv.at[h, 1], kv.at[h, 0], kv2_send.at[h], kv2_recv.at[h], d, (s + 1) % 4)

    def send_near(t):
        @pl.when(s < 3)
        def _():
            kv1(order(t)).start()

    def send_far(t):
        @pl.when(s == 0)
        def _():
            kv2(order(t)).start()

    send_near(0)
    send_far(0)
    seg1 = remote(seg_own, seg_all.at[1], seg_send.at[0], seg_recv.at[0], d, (s + 1) % 4)
    seg2 = remote(seg_own, seg_all.at[0], seg_send.at[1], seg_recv.at[1], d, (s + 2) % 4)

    @pl.when(s < 3)
    def _():
        seg1.start()

    @pl.when(s < 2)
    def _():
        seg2.start()

    og_copy.wait()
    ogs = remote(
        og.at[:, other], og2.at[pl.ds(toks, toks)], ogs_send, ogs_recv, d, sib
    )
    ogs.start()
    w_copy.wait()

    def grad_pair(i, c):
        at = pl.ds(pl.multiple_of(i * 2 * HEAD, 2 * HEAD), 2 * HEAD)
        g = dot(w[at, :], og[...], 1, 1).astype(BF16)
        dgrad[2 * i] = g[:HEAD]
        dgrad[2 * i + 1] = g[HEAD:]
        return c

    lax.fori_loop(0, heads // 2, grad_pair, 0)
    for t in range(1, AHEAD):
        send_near(t)
        send_far(t)

    @pl.when(s >= 1)
    def _():
        seg1.wait_recv()

    @pl.when(s >= 2)
    def _():
        seg2.wait_recv()

    down = lax.broadcasted_iota(jnp.int32, (toks, toks), 0)
    across = lax.broadcasted_iota(jnp.int32, (toks, toks), 1)
    row = seg_all[2][0:1, :]
    for j in range(3):
        column = jnp.sum(
            jnp.where(down == across, jnp.broadcast_to(seg_all[j][0:1, :], (toks, toks)), 0.0),
            axis=1, keepdims=True,
        )
        seen = column == row
        if j == 2:
            seen = seen & (down <= across)
        bias[j * toks:(j + 1) * toks, :] = jnp.where(seen, 0.0, -1e30)

    pltpu.make_async_copy(q_s, q_s, q_sem).wait()

    def attend(h):
        q = q_s[h]
        k3 = kv[h, :, 0].reshape(3 * toks, HEAD)
        v3 = kv[h, :, 1].reshape(3 * toks, HEAD)
        g = dgrad[h]
        score = dot(k3, q, 1, 1) * (HEAD ** -0.5 * LOG2E) + bias[...]
        raised = jnp.exp2(score - jnp.max(score, axis=0, keepdims=True))
        prob = raised * (1.0 / jnp.sum(raised, axis=0, keepdims=True))
        low = prob.astype(BF16)
        a = dot(v3, low, 0, 0).astype(BF16)
        att[h, :, 0:toks] = a
        att_copy(h).start()
        delta = jnp.sum(g.astype(F32) * a.astype(F32), axis=0, keepdims=True)
        change = (prob * (dot(v3, g, 1, 0) - delta)).astype(BF16)
        dq = dot(k3, change, 0, 0) * HEAD ** -0.5
        dq_out[:, lanes(h)] = dq.T.astype(BF16)
        dk = dot(change, q, 1, 0) * HEAD ** -0.5
        dv = dot(low, g, 1, 1)
        for i, term in enumerate((dk, dv)):
            dkv_own[h, i] = term[2 * toks:]
            dkv_out[h, 0, i] = term[toks:2 * toks].astype(BF16)
            dkv_out[h, 1, i] = term[:toks].astype(BF16)

    def att_copy(h):
        return remote(
            att.at[h, :, pl.ds(0, toks)], att.at[h, :, pl.ds(toks, toks)],
            att_send.at[h], att_recv.at[h], d, sib,
        )

    def back1(h):
        return remote(
            dkv_out.at[h, 0], dkv_in.at[0, h], dk1_send.at[h], dk1_recv.at[h], d, (s + 3) % 4
        )

    def back2(h):
        return remote(
            dkv_out.at[h, 1], dkv_in.at[1, h], dk2_send.at[h], dk2_recv.at[h], d,
            (s + 3 - (1 - core)) % 4,
        )

    def y_copy(h, j):
        to = (y + 1 + j) % RING
        return remote(
            part.at[h, pl.ds(pl.multiple_of(to * rows, rows), rows)], y_in.at[h, j],
            y_send.at[h, j], y_recv.at[h, j], place(z, to, hi), s,
        )

    def z_copy(t):
        h = order(t)
        slot = heads - 1 - apart(t)
        return remote(
            z_out.at[h], z_in.at[slot], z_send.at[slot], z_recv.at[slot], place(h, y, hi), s
        )

    def step(t, c):
        @pl.when((t < heads) & (s >= 1))
        def _():
            h = order(t)
            kv1(h).wait_recv()

            @pl.when(s == 2)
            def _():
                kv2_relay(h).start()

        @pl.when(t < heads)
        def _():
            h = order(t)

            @pl.when(s >= 2)
            def _():
                kv2(h).wait_recv()

            attend(h)

            @pl.when((s == 1) | (s == 3))
            def _():
                back1(h).start()

            @pl.when(s >= 2)
            def _():
                back2(h).start()

        @pl.when((t >= 1) & (t <= heads))
        def _():
            h = order(t - 1)
            att_copy(h).wait_recv()
            part[h] = dot(att[h], og2[...], 1, 0).astype(BF16)
            for j in range(RING - 1):
                y_copy(h, j).start()

        @pl.when((s == 2) & (t >= 2) & (t <= heads + 1))
        def _():
            h = order(t - 2)
            back2(h).wait_recv()
            dkv_out[h, 0] = (
                dkv_out[h, 0].astype(F32) + dkv_in[1, h].astype(F32)
            ).astype(BF16)
            back1(h).start()

        @pl.when(t < heads - AHEAD)
        def _():
            h = order(t)

            @pl.when(s < 3)
            def _():
                kv1(h).wait_send()

            @pl.when(s == 0)
            def _():
                kv2(h).wait_send()

            send_near(t + AHEAD)
            send_far(t + AHEAD)

        @pl.when(t >= LAG)
        def _():
            h = order(t - LAG)
            for j in range(RING - 1):
                y_copy(h, j).wait_recv()
            whole = part[h, pl.ds(pl.multiple_of(y * rows, rows), rows), :].astype(F32)
            for j in range(RING - 1):
                whole = whole + y_in[h, j].astype(F32)
            z_out[h] = whole.astype(BF16)

            @pl.when(t < heads + LAG - 1)
            def _():
                z_copy(t - LAG).start()

        return c

    og2_copy.wait()
    ogs.wait_recv()
    lax.fori_loop(0, heads + LAG, step, 0)

    total = z_out[z].astype(F32)
    for t in range(PLANES - 1):
        z_copy(t).wait_recv()
    for slot in range(PLANES - 1):
        total = total + z_in[slot].astype(F32)
    x_out[...] = total.astype(BF16)
    x_copies = []
    chip = hi * 2 + lo
    for i in range(1, 8):
        to = (chip + i // 2) % 4
        to_core = (core + i % 2) % 2
        piece = pl.ds(pl.multiple_of((to // 2) * share, share), share)
        copy = remote(
            x_out.at[piece], x_in.at[core, chip], x_send.at[i - 1], x_recv.at[core, chip],
            place(z, y, to // 2), (to % 2) * 2 + to_core,
        )
        copy.start()
        x_copies.append(copy)

    flat = att[:, :, 0:toks].reshape(heads * HEAD, toks).T
    width = proj_out.shape[1]
    span = min(512, width)

    def project(i, c):
        at = pl.ds(pl.multiple_of(i * span, span), span)
        proj_out[:, at] = dot(flat, w[:, at], 1, 0).astype(BF16)
        return c

    lax.fori_loop(0, width // span, project, 0)

    x_in[core, chip] = x_out[pl.ds(pl.multiple_of(hi * share, share), share), :]
    def finish(h, c):
        @pl.when(s < 3)
        def _():
            back1(h).wait_recv()

        @pl.when(s == 0)
        def _():
            back2(h).wait_recv()

        for i, out in enumerate((dk_out, dv_out)):
            @pl.when(s == 3)
            def _():
                out[:, lanes(h)] = dkv_own[h, i].astype(BF16)

            @pl.when((s == 1) | (s == 2))
            def _():
                out[:, lanes(h)] = (dkv_own[h, i] + dkv_in[0, h, i].astype(F32)).astype(BF16)

            @pl.when(s == 0)
            def _():
                out[:, lanes(h)] = (
                    dkv_own[h, i] + dkv_in[0, h, i].astype(F32) + dkv_in[1, h, i].astype(F32)
                ).astype(BF16)

        return c

    lax.fori_loop(0, heads, finish, 0)
    for i in range(1, 8):
        piece = x_in.at[(core + i % 2) % 2, (chip + i // 2) % 4]
        landed = x_recv.at[(core + i % 2) % 2, (chip + i // 2) % 4]
        pltpu.make_async_copy(piece, piece, landed).wait()
    for half in range(2):
        result = x_in[half, 0].astype(F32)
        for i in range(1, 4):
            result = result + x_in[half, i].astype(F32)
        wg_out[:, half * cols:(half + 1) * cols] = result.astype(BF16)

    def drain(h, c):
        @pl.when((s < 3) & (h >= heads - AHEAD))
        def _():
            kv1(order(h)).wait_send()

        @pl.when((s == 0) & (h >= heads - AHEAD))
        def _():
            kv2(order(h)).wait_send()

        @pl.when(s == 2)
        def _():
            kv2_relay(h).wait_send()

        @pl.when(s >= 1)
        def _():
            back1(h).wait_send()

        @pl.when(s >= 2)
        def _():
            back2(h).wait_send()

        att_copy(h).wait_send()
        for j in range(RING - 1):
            y_copy(h, j).wait_send()

        @pl.when(h < heads - 1)
        def _():
            z_copy(h).wait_send()

        return c

    lax.fori_loop(0, heads, drain, 0)
    ogs.wait_send()
    for copy in x_copies:
        copy.wait_send()

    @pl.when(s < 3)
    def _():
        seg1.wait_send()

    @pl.when(s < 2)
    def _():
        seg2.wait_send()


def settle(*refs):
    count = len(refs) // 2
    copies = [
        pltpu.make_async_copy(src, dst, refs[-1].at[i])
        for i, (src, dst) in enumerate(zip(refs[:count], refs[count:-1]))
    ]
    for copy in copies:
        copy.start()
    for copy in copies:
        copy.wait()


def body(queries, keys, values, segment_ids, out_weight, out_grad):
    toks, hd = queries.shape[1:]
    width = out_grad.shape[2]
    heads = hd // HEAD
    cols = width // 2
    rows = HEAD // RING
    share = rows // SIDES
    sem = pltpu.SemaphoreType.DMA
    any_space = pl.BlockSpec(memory_space=pl.ANY)
    in_vmem = pl.BlockSpec(memory_space=pltpu.VMEM)
    in_hbm = pl.BlockSpec(memory_space=pltpu.HBM)

    def stay(x):
        return pltpu.with_memory_space_constraint(x, pltpu.HBM)

    outs = pl.pallas_call(
        kernel,
        out_shape=(
            pltpu.VMEM((toks, width), BF16),
            pltpu.VMEM((toks, hd), BF16),
            pltpu.VMEM((toks, hd), BF16),
            pltpu.VMEM((toks, hd), BF16),
            pltpu.VMEM((share, width), BF16),
        ),
        in_specs=[in_hbm, in_hbm, in_hbm, in_vmem, in_hbm, in_hbm],
        out_specs=(in_vmem,) * 5,
        scratch_shapes=[
            pltpu.VMEM((heads, toks, HEAD), BF16),
            pltpu.VMEM((heads, 3, 2, toks, HEAD), BF16),
            pltpu.VMEM((toks, width), BF16),
            pltpu.VMEM((hd, width), BF16),
            pltpu.VMEM((2 * toks, cols), BF16),
            pltpu.VMEM((heads, HEAD, toks), BF16),
            pltpu.VMEM((heads, HEAD, 2 * toks), BF16),
            pltpu.VMEM((8, toks), F32),
            pltpu.VMEM((3, 8, toks), F32),
            pltpu.VMEM((3 * toks, toks), F32),
            pltpu.VMEM((heads, 2, toks, HEAD), F32),
            pltpu.VMEM((heads, 2, 2, toks, HEAD), BF16),
            pltpu.VMEM((2, heads, 2, toks, HEAD), BF16),
            pltpu.VMEM((heads, HEAD, cols), BF16),
            pltpu.VMEM((heads, RING - 1, rows, cols), BF16),
            pltpu.VMEM((heads, rows, cols), BF16),
            pltpu.VMEM((PLANES - 1, rows, cols), BF16),
            pltpu.VMEM((rows, cols), BF16),
            pltpu.VMEM((2, 4, share, cols), BF16),
            sem, sem((heads,)), sem, sem, sem, sem((2,)), sem((2,)), sem, sem,
            sem((heads,)), sem((heads,)), sem((heads,)), sem((heads,)),
            sem((heads,)), sem((heads,)), sem((heads,)), sem((heads,)),
            sem((heads,)), sem((heads,)), sem((heads, RING - 1)), sem((heads, RING - 1)),
            sem((PLANES - 1,)), sem((PLANES - 1,)),
            sem((7,)), sem((2, 4)),
        ],
        compiler_params=pltpu.CompilerParams(
            collective_id=0, has_side_effects=True, vmem_limit_bytes=54 << 20
        ),
        cost_estimate=pl.CostEstimate(
            flops=8 << 30, bytes_accessed=10 << 20, transcendentals=2 << 20
        ),
    )(
        stay(queries[0]), stay(keys[0]), stay(values[0]), segment_ids, stay(out_weight),
        stay(out_grad[0]),
    )
    outs = pl.pallas_call(
        settle,
        out_shape=tuple(jax.ShapeDtypeStruct(out.shape, out.dtype) for out in outs),
        in_specs=[in_vmem] * 5,
        out_specs=(any_space,) * 5,
        scratch_shapes=[sem((5,))],
        compiler_params=pltpu.CompilerParams(vmem_limit_bytes=4 << 20),
    )(*[pltpu.with_memory_space_constraint(out, pltpu.VMEM) for out in outs])
    return tuple(out[None] for out in outs[:4]) + (outs[4],)


def solution(mesh):
    placed = (
        P("dp", "seq", None),
        P("dp", "seq", None),
        P("dp", "seq", None),
        P("dp", "seq"),
        P(),
        P("dp", "seq", None),
    )
    return jax.shard_map(
        body,
        mesh=mesh,
        in_specs=placed,
        out_specs=placed[:1] * 4 + (P("dp", None),),
        check_vma=False,
    )
```

```python
import jax
import jax.numpy as jnp
from jax import lax
from jax.experimental import pallas as pl
from jax.experimental.pallas import tpu as pltpu
from jax.sharding import PartitionSpec as P

HEAD = 128
PLANES, RING, SIDES = 8, 4, 2
AHEAD = 3
LAG = 4
MESH = pl.DeviceIdType.MESH
F32, BF16 = jnp.float32, jnp.bfloat16
LOG2E = 1.4426950408889634


def dot(a, b, ca, cb):
    return lax.dot_general(a, b, (((ca,), (cb,)), ((), ())), preferred_element_type=F32)


def kernel(
    q_hbm, k_hbm, v_hbm, seg_ref, w_hbm, og_hbm,
    proj_out, dq_out, dk_out, dv_out, wg_out,
    q_s, kv, og, w, og2, dgrad, att, seg_own, seg_all, bias,
    dkv_own, dkv_out, dkv_in, part, y_in, z_out, z_in, x_out, x_in,
    q_sem, kv_sem, og_sem, w_sem, og2_sem, seg_send, seg_recv, ogs_send, ogs_recv,
    kv1_send, kv1_recv, kv2_send, kv2_recv, dk1_send, dk1_recv, dk2_send, dk2_recv,
    att_send, att_recv, y_send, y_recv, z_send, z_recv,
    x_send, x_recv,
):
    heads, toks = q_s.shape[0], q_s.shape[1]
    cols = og2.shape[1]
    rows = HEAD // RING
    share = rows // SIDES
    s = lax.axis_index("seq")
    d = lax.axis_index("dp")
    core = s % 2
    lo = s // 2
    z = d // (RING * SIDES)
    y = (d // SIDES) % RING
    hi = d % SIDES
    sib = s + 1 - 2 * core
    def place(zz, yy, xx):
        return zz * (RING * SIDES) + yy * SIDES + xx

    def remote(src, dst, send, recv, dp, seq):
        return pltpu.make_async_remote_copy(
            src_ref=src, dst_ref=dst, send_sem=send, recv_sem=recv,
            device_id=(dp, seq), device_id_type=MESH,
        )

    def lanes(h):
        return pl.ds(pl.multiple_of(h * HEAD, HEAD), HEAD)

    def apart(t):
        even = heads // 2 + t // 2
        odd = (heads - 1 - t) // 2
        return even + (t % 2) * (odd - even)

    def order(t):
        return (z + apart(t)) % heads

    barrier = pltpu.get_barrier_semaphore()
    peers = [(d, (s + 1) % 4), (d, (s + 2) % 4), (d, (s + 3) % 4)]
    peers += [(place(z, (y + i) % RING, hi), s) for i in range(1, RING)]
    peers += [(place((z + i) % PLANES, y, hi), s) for i in range(1, PLANES)]
    peers += [(place(z, y, 1 - hi), i) for i in range(4)]
    for peer in peers:
        pl.semaphore_signal(barrier, inc=1, device_id=peer, device_id_type=MESH)

    def load_head(i, c):
        h = order(i)
        pltpu.make_async_copy(k_hbm.at[:, lanes(h)], kv.at[h, 2, 0], kv_sem.at[h]).start()
        pltpu.make_async_copy(v_hbm.at[:, lanes(h)], kv.at[h, 2, 1], kv_sem.at[h]).start()
        return c

    lax.fori_loop(0, heads, load_head, 0)
    og_copy = pltpu.make_async_copy(og_hbm, og, og_sem)
    w_copy = pltpu.make_async_copy(w_hbm, w, w_sem)
    og_copy.start()
    w_copy.start()

    def load_query(i, c):
        pltpu.make_async_copy(q_hbm.at[:, lanes(i)], q_s.at[i], q_sem).start()
        return c

    lax.fori_loop(0, heads, load_query, 0)
    mine = pl.ds(pl.multiple_of(core * cols, cols), cols)
    other = pl.ds(pl.multiple_of((1 - core) * cols, cols), cols)
    og2_copy = pltpu.make_async_copy(og_hbm.at[:, mine], og2.at[pl.ds(0, toks)], og2_sem)
    og2_copy.start()

    seg_own[...] = jnp.broadcast_to(seg_ref[0:1, :].astype(F32), seg_own.shape)
    seg_all[2] = seg_own[...]

    @pl.when(s < 2)
    def _():
        seg_all[0] = jnp.full(seg_own.shape, -1.0, F32)

        def clear(h, c):
            kv[h, 0] = jnp.zeros((2, toks, HEAD), BF16)
            return c

        lax.fori_loop(0, heads, clear, 0)

    @pl.when(s < 1)
    def _():
        seg_all[1] = jnp.full(seg_own.shape, -1.0, F32)

        def clear(h, c):
            kv[h, 1] = jnp.zeros((2, toks, HEAD), BF16)
            return c

        lax.fori_loop(0, heads, clear, 0)

    def wait_head(h, c):
        pltpu.make_async_copy(kv.at[h, 2], kv.at[h, 2], kv_sem.at[h]).wait()
        return c

    lax.fori_loop(0, heads, wait_head, 0)
    pl.semaphore_wait(barrier, len(peers))

    def kv1(h):
        return remote(kv.at[h, 2], kv.at[h, 1], kv1_send.at[h], kv1_recv.at[h], d, (s + 1) % 4)

    def kv2(h):
        return remote(kv.at[h, 2], kv.at[h, 0], kv2_send.at[h], kv2_recv.at[h], d, (s + 2) % 4)

    def kv2_relay(h):
        return remote(kv.at[h, 1], kv.at[h, 0], kv2_send.at[h], kv2_recv.at[h], d, (s + 1) % 4)

    def send_near(t):
        @pl.when(s < 3)
        def _():
            kv1(order(t)).start()

    def send_far(t):
        @pl.when(s == 0)
        def _():
            kv2(order(t)).start()

    send_near(0)
    send_far(0)
    seg1 = remote(seg_own, seg_all.at[1], seg_send.at[0], seg_recv.at[0], d, (s + 1) % 4)
    seg2 = remote(seg_own, seg_all.at[0], seg_send.at[1], seg_recv.at[1], d, (s + 2) % 4)

    @pl.when(s < 3)
    def _():
        seg1.start()

    @pl.when(s < 2)
    def _():
        seg2.start()

    og_copy.wait()
    ogs = remote(
        og.at[:, other], og2.at[pl.ds(toks, toks)], ogs_send, ogs_recv, d, sib
    )
    ogs.start()
    w_copy.wait()

    def grad_pair(i, c):
        at = pl.ds(pl.multiple_of(i * 2 * HEAD, 2 * HEAD), 2 * HEAD)
        g = dot(w[at, :], og[...], 1, 1).astype(BF16)
        dgrad[2 * i] = g[:HEAD]
        dgrad[2 * i + 1] = g[HEAD:]
        return c

    lax.fori_loop(0, heads // 2, grad_pair, 0)
    for t in range(1, AHEAD):
        send_near(t)
        send_far(t)

    @pl.when(s >= 1)
    def _():
        seg1.wait_recv()

    @pl.when(s >= 2)
    def _():
        seg2.wait_recv()

    down = lax.broadcasted_iota(jnp.int32, (toks, toks), 0)
    across = lax.broadcasted_iota(jnp.int32, (toks, toks), 1)
    row = seg_all[2][0:1, :]
    for j in range(3):
        column = jnp.sum(
            jnp.where(down == across, jnp.broadcast_to(seg_all[j][0:1, :], (toks, toks)), 0.0),
            axis=1, keepdims=True,
        )
        seen = column == row
        if j == 2:
            seen = seen & (down <= across)
        bias[j * toks:(j + 1) * toks, :] = jnp.where(seen, 0.0, -1e30)

    pltpu.make_async_copy(q_s, q_s, q_sem).wait()

    def attend(h):
        q = q_s[h]
        k3 = kv[h, :, 0].reshape(3 * toks, HEAD)
        v3 = kv[h, :, 1].reshape(3 * toks, HEAD)
        g = dgrad[h]
        score = dot(k3, q, 1, 1) * (HEAD ** -0.5 * LOG2E) + bias[...]
        raised = jnp.exp2(score - jnp.max(score, axis=0, keepdims=True))
        prob = raised * (1.0 / jnp.sum(raised, axis=0, keepdims=True))
        low = prob.astype(BF16)
        a = dot(v3, low, 0, 0).astype(BF16)
        att[h, :, 0:toks] = a
        att_copy(h).start()
        delta = jnp.sum(g.astype(F32) * a.astype(F32), axis=0, keepdims=True)
        change = (prob * (dot(v3, g, 1, 0) - delta)).astype(BF16)
        dq = dot(k3, change, 0, 0) * HEAD ** -0.5
        dq_out[:, lanes(h)] = dq.T.astype(BF16)
        dk = dot(change, q, 1, 0) * HEAD ** -0.5
        dv = dot(low, g, 1, 1)
        for i, term in enumerate((dk, dv)):
            dkv_own[h, i] = term[2 * toks:]
            dkv_out[h, 0, i] = term[toks:2 * toks].astype(BF16)
            dkv_out[h, 1, i] = term[:toks].astype(BF16)

    def att_copy(h):
        return remote(
            att.at[h, :, pl.ds(0, toks)], att.at[h, :, pl.ds(toks, toks)],
            att_send.at[h], att_recv.at[h], d, sib,
        )

    def back1(h):
        return remote(
            dkv_out.at[h, 0], dkv_in.at[0, h], dk1_send.at[h], dk1_recv.at[h], d, (s + 3) % 4
        )

    def back2(h):
        return remote(
            dkv_out.at[h, 1], dkv_in.at[1, h], dk2_send.at[h], dk2_recv.at[h], d,
            (s + 3 - (1 - core)) % 4,
        )

    def y_copy(h, j):
        to = (y + 1 + j) % RING
        return remote(
            part.at[h, pl.ds(pl.multiple_of(to * rows, rows), rows)], y_in.at[h, j],
            y_send.at[h, j], y_recv.at[h, j], place(z, to, hi), s,
        )

    def z_copy(t):
        h = order(t)
        slot = heads - 1 - apart(t)
        return remote(
            z_out.at[h], z_in.at[slot], z_send.at[slot], z_recv.at[slot], place(h, y, hi), s
        )

    def step(t, c):
        @pl.when((t < heads) & (s >= 1))
        def _():
            h = order(t)
            kv1(h).wait_recv()

            @pl.when(s == 2)
            def _():
                kv2_relay(h).start()

        @pl.when(t < heads)
        def _():
            h = order(t)

            @pl.when(s >= 2)
            def _():
                kv2(h).wait_recv()

            attend(h)

            @pl.when((s == 1) | (s == 3))
            def _():
                back1(h).start()

            @pl.when(s >= 2)
            def _():
                back2(h).start()

        @pl.when((t >= 1) & (t <= heads))
        def _():
            h = order(t - 1)
            att_copy(h).wait_recv()
            part[h] = dot(att[h], og2[...], 1, 0).astype(BF16)
            for j in range(RING - 1):
                y_copy(h, j).start()

        @pl.when((s == 2) & (t >= 2) & (t <= heads + 1))
        def _():
            h = order(t - 2)
            back2(h).wait_recv()
            dkv_out[h, 0] = (
                dkv_out[h, 0].astype(F32) + dkv_in[1, h].astype(F32)
            ).astype(BF16)
            back1(h).start()

        @pl.when(t < heads - AHEAD)
        def _():
            h = order(t)

            @pl.when(s < 3)
            def _():
                kv1(h).wait_send()

            @pl.when(s == 0)
            def _():
                kv2(h).wait_send()

            send_near(t + AHEAD)
            send_far(t + AHEAD)

        @pl.when(t >= LAG)
        def _():
            h = order(t - LAG)
            for j in range(RING - 1):
                y_copy(h, j).wait_recv()
            whole = part[h, pl.ds(pl.multiple_of(y * rows, rows), rows), :].astype(F32)
            for j in range(RING - 1):
                whole = whole + y_in[h, j].astype(F32)
            z_out[h] = whole.astype(BF16)

            @pl.when(t < heads + LAG - 1)
            def _():
                z_copy(t - LAG).start()

        return c

    og2_copy.wait()
    ogs.wait_recv()
    lax.fori_loop(0, heads + LAG, step, 0)

    total = z_out[z].astype(F32)
    for t in range(PLANES - 1):
        z_copy(t).wait_recv()
    for slot in range(PLANES - 1):
        total = total + z_in[slot].astype(F32)
    x_out[...] = total.astype(BF16)
    x_copies = []
    chip = hi * 2 + lo
    for i in range(1, 8):
        to = (chip + i // 2) % 4
        to_core = (core + i % 2) % 2
        piece = pl.ds(pl.multiple_of((to // 2) * share, share), share)
        copy = remote(
            x_out.at[piece], x_in.at[core, chip], x_send.at[i - 1], x_recv.at[core, chip],
            place(z, y, to // 2), (to % 2) * 2 + to_core,
        )
        copy.start()
        x_copies.append(copy)

    flat = att[:, :, 0:toks].reshape(heads * HEAD, toks).T
    width = proj_out.shape[1]
    span = min(512, width)

    def project(i, c):
        at = pl.ds(pl.multiple_of(i * span, span), span)
        proj_out[:, at] = dot(flat, w[:, at], 1, 0).astype(BF16)
        return c

    lax.fori_loop(0, width // span, project, 0)

    x_in[core, chip] = x_out[pl.ds(pl.multiple_of(hi * share, share), share), :]
    def finish(h, c):
        @pl.when(s < 3)
        def _():
            back1(h).wait_recv()

        @pl.when(s == 0)
        def _():
            back2(h).wait_recv()

        for i, out in enumerate((dk_out, dv_out)):
            @pl.when(s == 3)
            def _():
                out[:, lanes(h)] = dkv_own[h, i].astype(BF16)

            @pl.when((s == 1) | (s == 2))
            def _():
                out[:, lanes(h)] = (dkv_own[h, i] + dkv_in[0, h, i].astype(F32)).astype(BF16)

            @pl.when(s == 0)
            def _():
                out[:, lanes(h)] = (
                    dkv_own[h, i] + dkv_in[0, h, i].astype(F32) + dkv_in[1, h, i].astype(F32)
                ).astype(BF16)

        return c

    lax.fori_loop(0, heads, finish, 0)
    for i in range(1, 8):
        piece = x_in.at[(core + i % 2) % 2, (chip + i // 2) % 4]
        landed = x_recv.at[(core + i % 2) % 2, (chip + i // 2) % 4]
        pltpu.make_async_copy(piece, piece, landed).wait()
    for half in range(2):
        result = x_in[half, 0].astype(F32)
        for i in range(1, 4):
            result = result + x_in[half, i].astype(F32)
        wg_out[:, half * cols:(half + 1) * cols] = result.astype(BF16)

    def drain(h, c):
        @pl.when((s < 3) & (h >= heads - AHEAD))
        def _():
            kv1(order(h)).wait_send()

        @pl.when((s == 0) & (h >= heads - AHEAD))
        def _():
            kv2(order(h)).wait_send()

        @pl.when(s == 2)
        def _():
            kv2_relay(h).wait_send()

        @pl.when(s >= 1)
        def _():
            back1(h).wait_send()

        @pl.when(s >= 2)
        def _():
            back2(h).wait_send()

        att_copy(h).wait_send()
        for j in range(RING - 1):
            y_copy(h, j).wait_send()

        @pl.when(h < heads - 1)
        def _():
            z_copy(h).wait_send()

        return c

    lax.fori_loop(0, heads, drain, 0)
    ogs.wait_send()
    for copy in x_copies:
        copy.wait_send()

    @pl.when(s < 3)
    def _():
        seg1.wait_send()

    @pl.when(s < 2)
    def _():
        seg2.wait_send()


def settle(*refs):
    count = len(refs) // 2
    copies = [
        pltpu.make_async_copy(src, dst, refs[-1].at[i])
        for i, (src, dst) in enumerate(zip(refs[:count], refs[count:-1]))
    ]
    for copy in copies:
        copy.start()
    for copy in copies:
        copy.wait()


def body(queries, keys, values, segment_ids, out_weight, out_grad):
    toks, hd = queries.shape[1:]
    width = out_grad.shape[2]
    heads = hd // HEAD
    cols = width // 2
    rows = HEAD // RING
    share = rows // SIDES
    sem = pltpu.SemaphoreType.DMA
    any_space = pl.BlockSpec(memory_space=pl.ANY)
    in_vmem = pl.BlockSpec(memory_space=pltpu.VMEM)
    in_hbm = pl.BlockSpec(memory_space=pltpu.HBM)

    def stay(x):
        return pltpu.with_memory_space_constraint(x, pltpu.HBM)

    outs = pl.pallas_call(
        kernel,
        out_shape=(
            pltpu.VMEM((toks, width), BF16),
            pltpu.VMEM((toks, hd), BF16),
            pltpu.VMEM((toks, hd), BF16),
            pltpu.VMEM((toks, hd), BF16),
            pltpu.VMEM((share, width), BF16),
        ),
        in_specs=[in_hbm, in_hbm, in_hbm, in_vmem, in_hbm, in_hbm],
        out_specs=(in_vmem,) * 5,
        scratch_shapes=[
            pltpu.VMEM((heads, toks, HEAD), BF16),
            pltpu.VMEM((heads, 3, 2, toks, HEAD), BF16),
            pltpu.VMEM((toks, width), BF16),
            pltpu.VMEM((hd, width), BF16),
            pltpu.VMEM((2 * toks, cols), BF16),
            pltpu.VMEM((heads, HEAD, toks), BF16),
            pltpu.VMEM((heads, HEAD, 2 * toks), BF16),
            pltpu.VMEM((8, toks), F32),
            pltpu.VMEM((3, 8, toks), F32),
            pltpu.VMEM((3 * toks, toks), F32),
            pltpu.VMEM((heads, 2, toks, HEAD), F32),
            pltpu.VMEM((heads, 2, 2, toks, HEAD), BF16),
            pltpu.VMEM((2, heads, 2, toks, HEAD), BF16),
            pltpu.VMEM((heads, HEAD, cols), BF16),
            pltpu.VMEM((heads, RING - 1, rows, cols), BF16),
            pltpu.VMEM((heads, rows, cols), BF16),
            pltpu.VMEM((PLANES - 1, rows, cols), BF16),
            pltpu.VMEM((rows, cols), BF16),
            pltpu.VMEM((2, 4, share, cols), BF16),
            sem, sem((heads,)), sem, sem, sem, sem((2,)), sem((2,)), sem, sem,
            sem((heads,)), sem((heads,)), sem((heads,)), sem((heads,)),
            sem((heads,)), sem((heads,)), sem((heads,)), sem((heads,)),
            sem((heads,)), sem((heads,)), sem((heads, RING - 1)), sem((heads, RING - 1)),
            sem((PLANES - 1,)), sem((PLANES - 1,)),
            sem((7,)), sem((2, 4)),
        ],
        compiler_params=pltpu.CompilerParams(
            collective_id=0, has_side_effects=True, vmem_limit_bytes=54 << 20
        ),
        cost_estimate=pl.CostEstimate(
            flops=8 << 30, bytes_accessed=10 << 20, transcendentals=2 << 20
        ),
    )(
        stay(queries[0]), stay(keys[0]), stay(values[0]), segment_ids, stay(out_weight),
        stay(out_grad[0]),
    )
    outs = pl.pallas_call(
        settle,
        out_shape=tuple(jax.ShapeDtypeStruct(out.shape, out.dtype) for out in outs),
        in_specs=[in_vmem] * 5,
        out_specs=(any_space,) * 5,
        scratch_shapes=[sem((5,))],
        compiler_params=pltpu.CompilerParams(vmem_limit_bytes=4 << 20),
    )(*[pltpu.with_memory_space_constraint(out, pltpu.VMEM) for out in outs])
    return tuple(out[None] for out in outs[:4]) + (outs[4],)


def solution(mesh):
    placed = (
        P("dp", "seq", None),
        P("dp", "seq", None),
        P("dp", "seq", None),
        P("dp", "seq"),
        P(),
        P("dp", "seq", None),
    )
    return jax.shard_map(
        body,
        mesh=mesh,
        in_specs=placed,
        out_specs=placed[:1] * 4 + (P("dp", None),),
        check_vma=False,
    )
```
